256 devices in a mesh: aux: 16 (over z, core), grp: 16 (over x, y).
Axes of the slice: x: 4, y: 4, z: 8, core: 2. Of those that a mesh axis runs over, the one named last changes fastest.
Arguments:
- integrals: bfloat16 [1024, 512, 256], P('aux', 'grp'), may hold values from -2.5 to 2.5
- metric: bfloat16 [1024, 1024], replicated, may hold values from -0.1875 to 0.1875
- fock: bfloat16 [512, 512], replicated, may hold values from -2 to 0.5, as said below
- virt_energy: float32 [256], replicated, may hold values from 0.3 to 3
- send_orb: int32 [256, 16], P(('aux', 'grp')), may hold values from 0 to 1, as said below
- pair_orb: int32 [4096, 2], P(('aux', 'grp')), may hold values from 0 to 511, as said below
- send_pair: int32 [256, 16], P(('aux', 'grp')), may hold values from 0 to 15, as said below
- cpl_slot: int32 [4096, 4], P(('aux', 'grp')), may hold values from 0 to 15, as said below
- cpl_orb: int32 [4096, 4, 2], P(('aux', 'grp')), may hold values from 0 to 511, as said below
Outputs:
- amplitudes: float32 [4096, 256, 256], P(('aux', 'grp'))
The draws below stay inside these ranges and needn't reach their ends.
Inputs may be any that keep to these rules, and one draw needn't show every extreme that they name: send_orb is below 2. `pair_orb`: the orbitals of the pairs owned by device (col, g) lie in column col: an orbital o of them has (o % 32) // 2 == col and o % 2 == send_orb[col * 16 + o // 32, g]. No pair is listed twice on a device. send_pair indexes the sending device's own pairs. `cpl_slot`: the entries of one pair are distinct. cpl_orb[p, e] equals pair_orb of the pair q[p, e] defined in the reference program. fock is symmetric with diagonal entries between -2 and -0.5.
All inputs are finite; a program needn't handle non-finite values.
Results may differ from the reference program's by a relative error of at most 0.0027.
Values may be sent and summed in bfloat16 or wider, within the bound.
No kernel may reach another device: no remote copies, remote signals or barrier semaphores. Data moves between devices by JAX's collectives and lax.ppermute only.
A program may use at most 128 MiB of HBM per device.

```python
import math
import jax
import jax.numpy as jnp
from jax import lax

NAUX = 1024
NOCC = 512
NV = 256
PAIRS = 16
NC = 4
ITERS = 2
N_AUX = 16
N_GRP = 16


def routing(key):
    base = jax.random.fold_in(key, 9173)
    keys = jax.random.split(base, 4)
    ndev = N_AUX * N_GRP
    orb_dev = NOCC // ndev
    group_orbs = NOCC // N_GRP
    grid = N_GRP * N_GRP
    send_orb = jax.random.randint(keys[0], (N_AUX, N_GRP, N_GRP), 0, orb_dev).astype(jnp.int32)
    col_base = jnp.arange(N_AUX, dtype=jnp.int32)[:, None, None] * orb_dev
    grp_base = jnp.arange(N_GRP, dtype=jnp.int32)[None, :, None] * group_orbs
    slot_orb = grp_base + col_base + send_orb
    received = jnp.transpose(slot_orb, (0, 2, 1))
    noise = jax.random.randint(keys[1], (N_AUX, N_GRP, grid), 0, 1 << 20)
    order = jnp.argsort(noise * grid + jnp.arange(grid, dtype=jnp.int32), axis=-1)[:, :, :PAIRS]
    orb_first = jnp.take_along_axis(received, order // N_GRP, axis=2)
    orb_second = jnp.take_along_axis(received, order % N_GRP, axis=2)
    left_i = orb_first[:, :, :, None, None]
    left_j = orb_second[:, :, :, None, None]
    right_k = orb_first[:, None, None, :, :]
    right_l = orb_second[:, None, None, :, :]
    share = (right_l == left_j) & (right_k != left_i) | (right_k == left_i) & (right_l != left_j)
    count = jnp.sum(share.astype(jnp.int32), axis=2)
    tie = jax.random.randint(keys[2], (N_AUX, N_GRP, N_GRP, PAIRS), 0, 1 << 10)
    score = count * (1 << 20) + tie * PAIRS + jnp.arange(PAIRS, dtype=jnp.int32)
    best = jnp.argmax(score, axis=-1).astype(jnp.int32)
    send_pair = jnp.transpose(best, (0, 2, 1))
    pick = best[..., None] == jnp.arange(PAIRS, dtype=jnp.int32)
    sent_first = jnp.sum(jnp.where(pick, orb_first[:, None, :, :], 0), axis=-1)
    sent_second = jnp.sum(jnp.where(pick, orb_second[:, None, :, :], 0), axis=-1)
    own_i = orb_first[..., None]
    own_j = orb_second[..., None]
    got_k = sent_first[:, :, None, :]
    got_l = sent_second[:, :, None, :]
    share_two = (got_l == own_j) & (got_k != own_i) | (got_k == own_i) & (got_l != own_j)
    tie_two = jax.random.randint(keys[3], (N_AUX, N_GRP, PAIRS, N_GRP), 0, 1 << 10)
    score_two = share_two.astype(jnp.int32) * (1 << 20) + tie_two * N_GRP + jnp.arange(N_GRP, dtype=jnp.int32)
    unused, chosen = lax.top_k(score_two, NC)
    chosen = chosen.astype(jnp.int32)
    shape_full = (N_AUX, N_GRP, PAIRS, N_GRP)
    cpl_first = jnp.take_along_axis(jnp.broadcast_to(got_k, shape_full), chosen, axis=3)
    cpl_second = jnp.take_along_axis(jnp.broadcast_to(got_l, shape_full), chosen, axis=3)
    pair_orb = jnp.stack([orb_first, orb_second], axis=-1).reshape(ndev * PAIRS, 2)
    cpl_orb = jnp.stack([cpl_first, cpl_second], axis=-1).reshape(ndev * PAIRS, NC, 2)
    return (send_orb.reshape(ndev, N_GRP).astype(jnp.int32), pair_orb.astype(jnp.int32), send_pair.reshape(ndev, N_GRP).astype(jnp.int32), chosen.reshape(ndev * PAIRS, NC), cpl_orb.astype(jnp.int32))


def draw_send_orb(key, part):
    return routing(key)[0]


def draw_pair_orb(key, part):
    return routing(key)[1]


def draw_send_pair(key, part):
    return routing(key)[2]


def draw_cpl_slot(key, part):
    return routing(key)[3]


def draw_cpl_orb(key, part):
    return routing(key)[4]


def draw_fock(key, part):
    base = jax.random.fold_in(key, 311)
    key_off, key_diag = jax.random.split(base)
    raw = jnp.clip(jax.random.normal(key_off, (NOCC, NOCC), jnp.float32), -4.0, 4.0) * 0.15
    symmetric = jnp.clip((raw + raw.T) * 0.7071, -0.5, 0.5)
    diag = -jax.random.uniform(key_diag, (NOCC,), jnp.float32, 0.5, 2.0)
    eye = jnp.eye(NOCC, dtype=jnp.float32)
    return (symmetric * (1.0 - eye) + eye * diag[None, :]).astype(jnp.bfloat16)


def steps_of(key, extent, cuts, smallest, largest):
    level, own = 1.0, jax.random.fold_in(key, 6)
    for position, blocks in cuts:
        steps = jnp.exp(jax.random.uniform(jax.random.fold_in(own, position), (blocks,), jnp.float32, smallest / len(cuts), largest / len(cuts)))
        level = level * jnp.repeat(steps, extent[position] // blocks).reshape([-1 if axis == position else 1 for axis in range(len(extent))])
    return level


def bell_draw(rng, dims, width, bound, cuts=(), held_as=jnp.bfloat16):
    factor_of = steps_of(rng, dims, cuts, -0.22, 0.18) if cuts else 1.0
    result = jax.random.normal(rng, dims, jnp.float32) * width * factor_of
    return jnp.minimum(jnp.maximum(result, -bound), bound).astype(held_as)


def setup_inputs(seed: int = 0) -> dict:
    seeds = jax.random.split(jax.random.key(seed), 10)
    integrals = bell_draw(seeds[0], (NAUX, NOCC, NV), (NAUX ** -0.25), 2.5, ((0, 16), (1, 16)))
    metric = bell_draw(seeds[1], (NAUX, NAUX), NAUX ** -0.5, 0.1875)
    fock = draw_fock(jax.random.fold_in(seeds[9], 71), 0)
    virt_energy = jnp.clip(jnp.exp(jax.random.uniform(seeds[3], (NV,), jnp.float32, math.log(0.3), math.log(3.0))), 0.3, 3.0)
    send_orb = draw_send_orb(jax.random.fold_in(seeds[9], 71), 0)
    pair_orb = draw_pair_orb(jax.random.fold_in(seeds[9], 71), 0)
    send_pair = draw_send_pair(jax.random.fold_in(seeds[9], 71), 0)
    cpl_slot = draw_cpl_slot(jax.random.fold_in(seeds[9], 71), 0)
    cpl_orb = draw_cpl_orb(jax.random.fold_in(seeds[9], 71), 0)
    return {"integrals": integrals, "metric": metric, "fock": fock, "virt_energy": virt_energy, "send_orb": send_orb, "pair_orb": pair_orb, "send_pair": send_pair, "cpl_slot": cpl_slot, "cpl_orb": cpl_orb}


def fitted_all(integrals, metric):
    flat = integrals.reshape(NAUX, NOCC * NV)
    fitted = jnp.dot(metric, flat, preferred_element_type=jnp.float32)
    return fitted.astype(jnp.bfloat16).reshape(NAUX, NOCC, NV)


def reference(integrals, metric, fock, virt_energy, send_orb, pair_orb, send_pair, cpl_slot, cpl_orb):
    fock = fock.astype(jnp.float32)
    ndev = N_AUX * N_GRP
    group_orbs = NOCC // N_GRP
    orb_dev = NOCC // ndev
    fitted = fitted_all(integrals, metric)
    device = (jnp.arange(ndev * PAIRS, dtype=jnp.int32) // PAIRS).astype(jnp.int32)
    column = device // N_GRP
    group = device % N_GRP

    def routed(orbital):
        source = orbital // group_orbs
        chosen = send_orb[column * N_GRP + source, group]
        return (source * group_orbs + column * orb_dev + chosen).astype(jnp.int32)

    orb_i = pair_orb[:, 0]
    orb_j = pair_orb[:, 1]
    src_i = routed(orb_i).reshape(ndev, PAIRS)
    src_j = routed(orb_j).reshape(ndev, PAIRS)

    def pair_block(args):
        left_idx, right_idx = args
        left = jnp.take(fitted, left_idx, axis=1).astype(jnp.float32)
        right = jnp.take(fitted, right_idx, axis=1).astype(jnp.float32)
        return jnp.einsum("qpa,qpb->pab", left, right)

    kmat = lax.map(pair_block, (src_i, src_j))
    diag_sum = (fock[orb_i, orb_i] + fock[orb_j, orb_j]).reshape(ndev, PAIRS)

    k_orb = cpl_orb[:, :, 0]
    l_orb = cpl_orb[:, :, 1]
    first = (l_orb == orb_j[:, None]) & (k_orb != orb_i[:, None])
    second = (k_orb == orb_i[:, None]) & (l_orb != orb_j[:, None])
    f_ik = fock[orb_i[:, None], k_orb]
    f_jl = fock[orb_j[:, None], l_orb]
    weight = (jnp.where(first, f_ik, jnp.float32(0.0)) + jnp.where(second, f_jl, jnp.float32(0.0))).reshape(ndev, PAIRS, NC)

    dev_ids = jnp.arange(ndev, dtype=jnp.int32)
    dev_col = dev_ids // N_GRP
    dev_grp = dev_ids % N_GRP
    sender = (dev_col[:, None] * N_GRP + jnp.arange(N_GRP, dtype=jnp.int32)[None, :]).astype(jnp.int32)
    qtab = (sender * PAIRS + send_pair[sender, dev_grp[:, None]]).astype(jnp.int32)
    slots = cpl_slot.reshape(ndev, PAIRS, NC)
    qpair = jnp.take_along_axis(jnp.broadcast_to(qtab[:, None, :], (ndev, PAIRS, N_GRP)), slots, axis=2)

    def denominator(dsum):
        return (virt_energy[:, None] + virt_energy[None, :])[None, :, :] - dsum[:, None, None]

    def start(args):
        kblk, dsum = args
        return -(kblk / denominator(dsum))

    amps = lax.map(start, (kmat, diag_sum))
    for step in range(ITERS):
        rounded = amps.astype(jnp.bfloat16).reshape(ndev * PAIRS, NV, NV)

        def update(args):
            kblk, ablk, dsum, wblk, qrow = args
            den = denominator(dsum)
            coupled = jnp.take(rounded, qrow.reshape(-1), axis=0).astype(jnp.float32).reshape(PAIRS, NC, NV, NV)
            term = jnp.einsum("pc,pcab->pab", wblk, coupled)
            resid = kblk + den * ablk - term
            return ablk - resid / den

        amps = lax.map(update, (kmat, amps, diag_sum, weight, qpair))
    return amps.reshape(ndev * PAIRS, NV, NV)
```

```python
import jax
import jax.numpy as jnp
from jax import lax
from jax.experimental import pallas as pl
from jax.experimental.pallas import tpu as pltpu
from jax.sharding import PartitionSpec as P

NT = (((1,), (1,)), ((), ()))


def recip(x):
    r = pl.reciprocal(x, approx=True)
    return r * (2.0 - x * r)


def pair_kernel(idx, slot, wts, dsum, pool, vrow, vcol, out, vsum, acc, amp):
    t = pl.program_id(0)

    @pl.when(t == 0)
    def _():
        vsum[...] = vrow[...] + vcol[...]

    def kmat(n):
        return lax.dot_general(
            pool[idx[n, 0]], pool[idx[n, 1]], NT, preferred_element_type=jnp.float32
        )

    @pl.when(t < 16)
    def _():
        acc[...] = -kmat(16 + t)

        def entry(e, carry):
            n = 4 * t + e

            @pl.when(wts[64 + n] != 0.0)
            def _():
                start = -(kmat(32 + n) * recip(vsum[...] - dsum[32 + n]))
                rounded = start.astype(jnp.bfloat16).astype(jnp.float32)
                acc[...] += wts[64 + n] * rounded

            return carry

        lax.fori_loop(0, 4, entry, 0)
        amp[t] = (acc[...] * recip(vsum[...] - dsum[16 + t])).astype(jnp.bfloat16)

    @pl.when(t >= 16)
    def _():
        p = t - 16
        total = -kmat(p)
        for e in range(4):
            total += wts[4 * p + e] * amp[slot[4 * p + e]].astype(jnp.float32)
        out[0] = total * recip(vsum[...] - dsum[p])


def local_orbital(orbital):
    return orbital // 32 * 2 + orbital % 2


def lookup(table, rows, cols):
    ids = jnp.arange(32, dtype=jnp.int32)
    pick = (rows[:, None, None] == ids[None, :, None]) & (
        cols[:, None, None] == ids[None, None, :]
    )
    return jnp.sum(jnp.where(pick, table[None], 0.0), axis=(1, 2))


def coupling(table, orb, cpl):
    i, j = orb[:, 0, None], orb[:, 1, None]
    k, l = cpl[:, :, 0], cpl[:, :, 1]
    first = (l == j) & (k != i)
    second = (k == i) & (l != j)
    rows = jnp.where(first, i, j) + jnp.zeros_like(k)
    cols = jnp.where(first, k, l)
    value = lookup(table, rows.reshape(-1), cols.reshape(-1)).reshape(k.shape)
    return jnp.where(first | second, value, 0.0).reshape(-1)


def on_device(
    integrals, metric, fock, virt_energy, send_orb, pair_orb, send_pair, cpl_slot, cpl_orb
):
    col = lax.axis_index("aux")
    grp = lax.axis_index("grp")
    orb = local_orbital(pair_orb)
    cpl = local_orbital(cpl_orb)
    meta = jnp.concatenate([orb.reshape(16, 2), cpl.reshape(16, 8)], axis=1)
    meta = jnp.concatenate([meta.reshape(1, 160), send_pair], axis=1)
    metas = lax.all_gather(meta, "grp", axis=0, tiled=True)
    chosen = jnp.sum(
        jnp.where(jnp.arange(16)[None, :] == grp, metas[:, 160:], 0), axis=1
    )
    pick = chosen[:, None, None] == jnp.arange(16, dtype=jnp.int32)[None, :, None]
    sent = jnp.sum(jnp.where(pick, metas[:, :160].reshape(16, 16, 10), 0), axis=1)
    orb_q, cpl_q = sent[:, :2], sent[:, 2:].reshape(16, 4, 2)

    local = jnp.arange(32, dtype=jnp.int32)
    whole = local // 2 * 32 + col * 2 + local % 2
    select = (whole[:, None] == jnp.arange(512)[None, :]).astype(jnp.bfloat16)
    fock_rows = jnp.dot(select, fock, preferred_element_type=jnp.float32)
    fock_col = lax.dot_general(
        fock_rows.astype(jnp.bfloat16), select, NT, preferred_element_type=jnp.float32
    )
    diag = jnp.sum(jnp.where(local[:, None] == local[None, :], fock_col, 0.0), axis=1)

    idx = jnp.concatenate([orb, orb_q, cpl_q.reshape(64, 2)], axis=0)
    at = idx[:, :, None] == local[None, None, :]
    dsum = jnp.sum(jnp.where(at, diag[None, None, :], 0.0), axis=2)
    dsum = dsum[:, 0] + dsum[:, 1]
    wts = jnp.concatenate([coupling(fock_col, orb, cpl), coupling(fock_col, orb_q, cpl_q)])

    rows = integrals.reshape(64, 16, 512).transpose(1, 0, 2)
    block = lax.all_to_all(rows, "aux", split_axis=0, concat_axis=0, tiled=True)
    fitted = lax.dot_general(
        block.reshape(1024, 512),
        metric,
        (((0,), (1,)), ((), ())),
        preferred_element_type=jnp.float32,
    ).astype(jnp.bfloat16)
    pool = lax.all_gather(fitted, "grp", axis=0, tiled=True).reshape(32, 256, 1024)

    smem = pl.BlockSpec(memory_space=pltpu.SMEM)
    vmem = pl.BlockSpec(memory_space=pltpu.VMEM)
    return pl.pallas_call(
        pair_kernel,
        grid=(32,),
        in_specs=[smem] * 4 + [vmem] * 3,
        out_specs=pl.BlockSpec((1, 256, 256), lambda t: (jnp.maximum(t - 16, 0), 0, 0)),
        out_shape=jax.ShapeDtypeStruct((16, 256, 256), jnp.float32),
        scratch_shapes=[
            pltpu.VMEM((256, 256), jnp.float32),
            pltpu.VMEM((256, 256), jnp.float32),
            pltpu.VMEM((16, 256, 256), jnp.bfloat16),
        ],
        compiler_params=pltpu.CompilerParams(vmem_limit_bytes=48 * 2**20),
    )(idx, cpl_slot.reshape(64), wts, dsum, pool, virt_energy[None, :], virt_energy[:, None])


def solution(mesh):
    in_specs = (
        P("aux", "grp", None),
        P(),
        P(),
        P(),
        P(("aux", "grp"), None),
        P(("aux", "grp"), None),
        P(("aux", "grp"), None),
        P(("aux", "grp"), None),
        P(("aux", "grp"), None, None),
    )
    out_specs = P(("aux", "grp"), None, None)
    return jax.shard_map(
        on_device, mesh=mesh, in_specs=in_specs, out_specs=out_specs, check_vma=False
    )
```

```python
import jax
import jax.numpy as jnp
from jax import lax
from jax.experimental import pallas as pl
from jax.experimental.pallas import tpu as pltpu
from jax.sharding import PartitionSpec as P

NT = (((1,), (1,)), ((), ()))
MIB = 2**20
MASKS = ((4, 12, 1, 3), (12, 4, 3, 1), (1, 3, 4, 12), (3, 1, 12, 4))


def recip(x):
    r = pl.reciprocal(x, approx=True)
    return r * (2.0 - x * r)


def listed(wts, order):
    def entry(n, count):
        hit = wts[64 + n] != 0.0

        @pl.when(hit)
        def _():
            order[count] = n

        return count + hit.astype(jnp.int32)

    count = lax.fori_loop(0, 64, entry, 0)
    for k in range(4):

        @pl.when(count + k < 64)
        def _(k=k):
            order[count + k] = -1

    return (count + 3) // 4


def load(pieces, pool, sems):
    copies = []
    for q in range(4):
        for part in range(2):
            copies.append(
                pltpu.make_async_copy(
                    pieces[2 * q + part], pool.at[q, pl.ds(16 * part, 16)], sems.at[2 * q + part]
                )
            )
    for copy in copies:
        copy.start()
    for copy in copies:
        copy.wait()


def product(idx, pool, n):
    left = jnp.concatenate([pool[q, idx[q, n]] for q in range(4)], axis=1)
    right = jnp.concatenate([pool[q, idx[q, 96 + n]] for q in range(4)], axis=1)
    return lax.dot_general(left, right, NT, preferred_element_type=jnp.float32)


def first_kernel(idx, wts, *refs):
    pieces, sums, pool, acc, order, sems, out_sems = refs[:8], *refs[8:]
    fours = listed(wts, order)
    load(pieces, pool, sems)

    def out_copy(g):
        rows = pl.ds(4 * g, 4)
        return pltpu.make_async_copy(acc.at[rows], sums.at[rows], out_sems.at[g])

    def plain(g, carry):
        for u in range(4):
            acc[4 * g + u] = product(idx, pool, 4 * g + u)
        out_copy(g).start()
        return carry

    def coupled(g, carry):
        for u in range(4):
            acc[32 + 4 * g + u] = product(idx, pool, 32 + jnp.maximum(order[4 * g + u], 0))
        out_copy(8 + g).start()
        return carry

    def finish(g, carry):
        out_copy(g).wait()
        return carry

    lax.fori_loop(0, 8, plain, 0)
    lax.fori_loop(0, fours, coupled, 0)
    lax.fori_loop(0, 8 + fours, finish, 0)


def last_kernel(idx, wts, slot, dsum, vrow, vcol, *refs):
    pieces, sums, out, pool, acc, mixed, amp, vsum, order, sems, in_sems = refs[:8], *refs[8:]
    fours = listed(wts, order)

    def in_copy(g):
        rows = pl.ds(4 * g, 4)
        return pltpu.make_async_copy(sums.at[rows], acc.at[rows], in_sems.at[g])

    def out_copy(g):
        rows = pl.ds(4 * g, 4)
        return pltpu.make_async_copy(acc.at[rows], out.at[rows], in_sems.at[g])

    def begin(g, carry):
        in_copy(g).start()
        return carry

    def clear(s, carry):
        mixed[s] = jnp.zeros((256, 256), jnp.float32)
        return carry

    lax.fori_loop(8, 8 + fours, begin, 0)
    lax.fori_loop(0, 8, begin, 0)
    vsum[...] = vrow[...] + vcol[...]
    lax.fori_loop(0, 16, clear, 0)
    load(pieces, pool, sems)

    def coupled(g, carry):
        in_copy(8 + g).wait()
        for u in range(4):
            entry = order[4 * g + u]
            n = jnp.maximum(entry, 0)
            weight = jnp.where(entry >= 0, wts[64 + n], 0.0)
            kmat = acc[32 + 4 * g + u] + product(idx, pool, 32 + n)
            start = -(kmat * recip(vsum[...] - dsum[32 + n]))
            rounded = start.astype(jnp.bfloat16).astype(jnp.float32)
            mixed[n // 4] += weight * rounded
        return carry

    def received(g, carry):
        in_copy(4 + g).wait()
        for u in range(4):
            s = 4 * g + u
            kmat = acc[16 + s] + product(idx, pool, 16 + s)
            value = (mixed[s] - kmat) * recip(vsum[...] - dsum[16 + s])
            amp[s] = value.astype(jnp.bfloat16)
        return carry

    def own(g, carry):
        in_copy(g).wait()
        for u in range(4):
            p = 4 * g + u
            total = -(acc[p] + product(idx, pool, p))
            for e in range(4):
                total += wts[4 * p + e] * amp[slot[4 * p + e]].astype(jnp.float32)
            acc[p] = total * recip(vsum[...] - dsum[p])
        out_copy(g).start()
        return carry

    def finish(g, carry):
        out_copy(g).wait()
        return carry

    lax.fori_loop(0, fours, coupled, 0)
    lax.fori_loop(0, 4, received, 0)
    lax.fori_loop(0, 4, own, 0)
    lax.fori_loop(0, 4, finish, 0)


SMEM = pl.BlockSpec(memory_space=pltpu.SMEM)
VMEM = pl.BlockSpec(memory_space=pltpu.VMEM)
HBM = pl.BlockSpec(memory_space=pl.ANY)


def first_sums(idx, wts, pieces):
    return pl.pallas_call(
        first_kernel,
        in_specs=[SMEM] * 2 + [HBM] * 8,
        out_specs=HBM,
        out_shape=jax.ShapeDtypeStruct((96, 256, 256), jnp.float32),
        scratch_shapes=[
            pltpu.VMEM((4, 32, 256, 128), jnp.bfloat16),
            pltpu.VMEM((96, 256, 256), jnp.float32),
            pltpu.SMEM((68,), jnp.int32),
            pltpu.SemaphoreType.DMA((8,)),
            pltpu.SemaphoreType.DMA((24,)),
        ],
        compiler_params=pltpu.CompilerParams(vmem_limit_bytes=44 * MIB),
        cost_estimate=pl.CostEstimate(
            flops=96 * 2 * 256 * 256 * 512, bytes_accessed=32 * MIB, transcendentals=0
        ),
    )(idx, wts, *pieces)


def amplitudes(idx, wts, slot, dsum, virt, pieces, sums):
    return pl.pallas_call(
        last_kernel,
        in_specs=[SMEM] * 4 + [VMEM] * 2 + [HBM] * 9,
        out_specs=HBM,
        out_shape=jax.ShapeDtypeStruct((16, 256, 256), jnp.float32),
        scratch_shapes=[
            pltpu.VMEM((4, 32, 256, 128), jnp.bfloat16),
            pltpu.VMEM((96, 256, 256), jnp.float32),
            pltpu.VMEM((16, 256, 256), jnp.float32),
            pltpu.VMEM((16, 256, 256), jnp.bfloat16),
            pltpu.VMEM((256, 256), jnp.float32),
            pltpu.SMEM((68,), jnp.int32),
            pltpu.SemaphoreType.DMA((8,)),
            pltpu.SemaphoreType.DMA((24,)),
        ],
        compiler_params=pltpu.CompilerParams(vmem_limit_bytes=52 * MIB),
        cost_estimate=pl.CostEstimate(
            flops=96 * 2 * 256 * 256 * 512, bytes_accessed=36 * MIB, transcendentals=0
        ),
    )(idx, wts, slot, dsum, virt[None, :], virt[:, None], *pieces, sums)


def lookup(table, rows, cols):
    ids = jnp.arange(32, dtype=jnp.int32)
    pick = (rows[:, None, None] == ids[None, :, None]) & (
        cols[:, None, None] == ids[None, None, :]
    )
    return jnp.sum(jnp.where(pick, table[None], 0.0), axis=(1, 2))


def coupling(table, orb, cpl):
    i, j = orb[:, 0, None], orb[:, 1, None]
    k, l = cpl[:, :, 0], cpl[:, :, 1]
    first = (l == j) & (k != i)
    second = (k == i) & (l != j)
    rows = jnp.where(first, i, j) + jnp.zeros_like(k)
    cols = jnp.where(first, k, l)
    value = lookup(table, rows.reshape(-1), cols.reshape(-1)).reshape(k.shape)
    return jnp.where(first | second, value, 0.0).reshape(-1)


def arrival(masks):
    order = [0]
    for mask in masks:
        order = order + [o ^ mask for o in order]
    return order


def tables(metas, fock, orb, cpl):
    col = lax.axis_index("aux")
    grp = lax.axis_index("grp")
    chosen = jnp.sum(
        jnp.where(jnp.arange(16)[None, :] == grp, metas[:, 160:], 0), axis=1
    )
    pick = chosen[:, None, None] == jnp.arange(16, dtype=jnp.int32)[None, :, None]
    sent = jnp.sum(jnp.where(pick, metas[:, :160].reshape(16, 16, 10), 0), axis=1)
    orb_q, cpl_q = sent[:, :2], sent[:, 2:].reshape(16, 4, 2)

    local = jnp.arange(32, dtype=jnp.int32)
    whole = local // 2 * 32 + col * 2 + local % 2
    select = (whole[:, None] == jnp.arange(512)[None, :]).astype(jnp.bfloat16)
    fock_rows = jnp.dot(select, fock, preferred_element_type=jnp.float32)
    fock_col = lax.dot_general(
        fock_rows.astype(jnp.bfloat16), select, NT, preferred_element_type=jnp.float32
    )
    diag = jnp.sum(jnp.where(local[:, None] == local[None, :], fock_col, 0.0), axis=1)

    orbs = jnp.concatenate([orb, orb_q, cpl_q.reshape(64, 2)], axis=0)
    at = orbs[:, :, None] == local[None, None, :]
    dsum = jnp.sum(jnp.where(at, diag[None, None, :], 0.0), axis=2)
    dsum = dsum[:, 0] + dsum[:, 1]
    wts = jnp.concatenate([coupling(fock_col, orb, cpl), coupling(fock_col, orb_q, cpl_q)])

    flat = orbs.T.reshape(1, 192)
    offset = (flat // 2) ^ grp
    place = jnp.array([arrival(m) for m in MASKS], jnp.int32)
    found = offset[:, :, None] == place[:, None, :]
    spot = jnp.sum(jnp.where(found, jnp.arange(16, dtype=jnp.int32), 0), axis=2)
    return spot * 2 + flat % 2, wts, dsum


def swap(block, mask):
    return lax.ppermute(block, "grp", [(g, g ^ mask) for g in range(16)])


def on_device(
    integrals, metric, fock, virt_energy, send_orb, pair_orb, send_pair, cpl_slot, cpl_orb
):
    orb = pair_orb // 32 * 2 + pair_orb % 2
    cpl = cpl_orb // 32 * 2 + cpl_orb % 2
    meta = jnp.concatenate([orb, cpl.reshape(16, 8)], axis=1).reshape(1, 160)
    meta = jnp.concatenate([meta, send_pair], axis=1)
    metas = lax.all_gather(meta, "grp", axis=0, tiled=True)

    rows = integrals.reshape(64, 16, 512).transpose(1, 0, 2)
    rows, metas = lax.optimization_barrier((rows, metas))
    idx, wts, dsum = tables(metas, fock, orb, cpl)
    block = lax.all_to_all(rows, "aux", split_axis=0, concat_axis=0, tiled=True)
    fitted = lax.dot_general(
        block.reshape(1024, 512),
        metric,
        (((0,), (1,)), ((), ())),
        preferred_element_type=jnp.float32,
    ).astype(jnp.bfloat16)
    held = [
        jnp.stack([fitted[:, 256 * q + 128 * h : 256 * q + 128 * h + 128] for h in range(2)])[:, None]
        for q in range(4)
    ]
    for step in range(3):
        got = [swap(held[q], MASKS[q][step]) for q in range(4)]
        held = [jnp.concatenate([a, b], axis=1) for a, b in zip(held, got)]
        held = list(lax.optimization_barrier(tuple(held)))
    halves = []
    for h in range(2):
        sent = [block[h] for block in held]
        got = [swap(sent[q], MASKS[q][3]) for q in range(4)]
        halves.append([x.reshape(16, 256, 128) for pair in zip(sent, got) for x in pair])
    sums = first_sums(idx, wts, halves[0])
    return amplitudes(idx, wts, cpl_slot.reshape(64), dsum, virt_energy, halves[1], sums)


def solution(mesh):
    in_specs = (
        P("aux", "grp", None),
        P(),
        P(),
        P(),
        P(("aux", "grp"), None),
        P(("aux", "grp"), None),
        P(("aux", "grp"), None),
        P(("aux", "grp"), None),
        P(("aux", "grp"), None, None),
    )
    out_specs = P(("aux", "grp"), None, None)
    return jax.shard_map(
        on_device, mesh=mesh, in_specs=in_specs, out_specs=out_specs, check_vma=False
    )
```

```python
import jax
import jax.numpy as jnp
from jax import lax
from jax.experimental import pallas as pl
from jax.experimental.pallas import tpu as pltpu
from jax.sharding import PartitionSpec as P

NT = (((1,), (1,)), ((), ()))
MIB = 2**20
MASKS = ((4, 12, 1, 3), (1, 3, 4, 12), (12, 4, 3, 1), (3, 1, 12, 4))


def recip(x):
    r = pl.reciprocal(x, approx=True)
    return r * (2.0 - x * r)


def listed(wts, order):
    def entry(n, count):
        hit = wts[64 + n] != 0.0

        @pl.when(hit)
        def _():
            order[count] = n

        return count + hit.astype(jnp.int32)

    count = lax.fori_loop(0, 64, entry, 0)
    for k in range(4):
        order[count + k] = -1
    return (count + 3) // 4


def pair_kernel(idx, wts, slot, dsum, vrow, vcol, *refs):
    pieces, out, pool, mixed, amp, vsum, order, sems, out_sems = refs[:16], *refs[16:]
    copies = [
        pltpu.make_async_copy(
            pieces[4 * q + part], pool.at[q, pl.ds(8 * part, 8)], sems.at[4 * q + part]
        )
        for q in range(4)
        for part in range(4)
    ]
    for copy in copies:
        copy.start()
    fours = listed(wts, order)
    vsum[...] = vrow[...] + vcol[...]

    def clear(s, carry):
        mixed[s] = jnp.zeros((256, 256), jnp.float32)
        return carry

    lax.fori_loop(0, 16, clear, 0)
    for copy in copies:
        copy.wait()

    def product(n):
        left = jnp.concatenate([pool[q, idx[q, n]] for q in range(4)], axis=1)
        right = jnp.concatenate([pool[q, idx[q, 96 + n]] for q in range(4)], axis=1)
        return lax.dot_general(left, right, NT, preferred_element_type=jnp.float32)

    def coupled(g, carry):
        for u in range(4):
            entry = order[4 * g + u]
            n = jnp.maximum(entry, 0)
            weight = jnp.where(entry >= 0, wts[64 + n], 0.0)
            start = -(product(32 + n) * recip(vsum[...] - dsum[32 + n]))
            rounded = start.astype(jnp.bfloat16).astype(jnp.float32)
            mixed[n // 4] += weight * rounded
        return carry

    def received(g, carry):
        for u in range(4):
            s = 4 * g + u
            value = (mixed[s] - product(16 + s)) * recip(vsum[...] - dsum[16 + s])
            amp[s] = value.astype(jnp.bfloat16)
        return carry

    def out_copy(g):
        rows = pl.ds(4 * g, 4)
        return pltpu.make_async_copy(mixed.at[rows], out.at[rows], out_sems.at[g])

    def own(g, carry):
        for u in range(4):
            p = 4 * g + u
            total = -product(p)
            for e in range(4):
                total += wts[4 * p + e] * amp[slot[4 * p + e]].astype(jnp.float32)
            mixed[p] = total * recip(vsum[...] - dsum[p])
        out_copy(g).start()
        return carry

    def finish(g, carry):
        out_copy(g).wait()
        return carry

    lax.fori_loop(0, fours, coupled, 0)
    lax.fori_loop(0, 4, received, 0)
    lax.fori_loop(0, 4, own, 0)
    lax.fori_loop(0, 4, finish, 0)


SMEM = pl.BlockSpec(memory_space=pltpu.SMEM)
VMEM = pl.BlockSpec(memory_space=pltpu.VMEM)
HBM = pl.BlockSpec(memory_space=pl.ANY)


def amplitudes(idx, wts, slot, dsum, virt, pieces):
    return pl.pallas_call(
        pair_kernel,
        in_specs=[SMEM] * 4 + [VMEM] * 2 + [HBM] * 16,
        out_specs=HBM,
        out_shape=jax.ShapeDtypeStruct((16, 256, 256), jnp.float32),
        scratch_shapes=[
            pltpu.VMEM((4, 32, 256, 256), jnp.bfloat16),
            pltpu.VMEM((16, 256, 256), jnp.float32),
            pltpu.VMEM((16, 256, 256), jnp.bfloat16),
            pltpu.VMEM((256, 256), jnp.float32),
            pltpu.SMEM((68,), jnp.int32),
            pltpu.SemaphoreType.DMA((16,)),
            pltpu.SemaphoreType.DMA((4,)),
        ],
        compiler_params=pltpu.CompilerParams(vmem_limit_bytes=58 * MIB),
        cost_estimate=pl.CostEstimate(
            flops=96 * 2 * 256 * 256 * 1024, bytes_accessed=20 * MIB, transcendentals=0
        ),
    )(idx, wts, slot, dsum, virt[None, :], virt[:, None], *pieces)


def lookup(table, rows, cols):
    ids = jnp.arange(32, dtype=jnp.int32)
    pick = (rows[:, None, None] == ids[None, :, None]) & (
        cols[:, None, None] == ids[None, None, :]
    )
    return jnp.sum(jnp.where(pick, table[None], 0.0), axis=(1, 2))


def coupling(table, orb, cpl):
    i, j = orb[:, 0, None], orb[:, 1, None]
    k, l = cpl[:, :, 0], cpl[:, :, 1]
    first = (l == j) & (k != i)
    second = (k == i) & (l != j)
    rows = jnp.where(first, i, j) + jnp.zeros_like(k)
    cols = jnp.where(first, k, l)
    value = lookup(table, rows.reshape(-1), cols.reshape(-1)).reshape(k.shape)
    return jnp.where(first | second, value, 0.0).reshape(-1)


def arrival(masks):
    order = [0]
    for mask in masks:
        order = order + [o ^ mask for o in order]
    return order


def found_in(values, order):
    ids = jnp.arange(16, dtype=jnp.int32)
    hit = values[..., None] == jnp.array(order, jnp.int32)
    return jnp.sum(jnp.where(hit, ids, 0), axis=-1)


def tables(metas, fock, orb, cpl, cpl_slot):
    col = lax.axis_index("aux")
    grp = lax.axis_index("grp")
    chosen = jnp.sum(
        jnp.where(jnp.arange(16)[None, :] == grp, metas[:, 160:], 0), axis=1
    )
    pick = chosen[:, None, None] == jnp.arange(16, dtype=jnp.int32)[None, :, None]
    sent = jnp.sum(jnp.where(pick, metas[:, :160].reshape(16, 16, 10), 0), axis=1)
    orb_q, cpl_q = sent[:, :2], sent[:, 2:].reshape(16, 4, 2)

    local = jnp.arange(32, dtype=jnp.int32)
    whole = local // 2 * 32 + col * 2 + local % 2
    select = (whole[:, None] == jnp.arange(512)[None, :]).astype(jnp.bfloat16)
    fock_rows = jnp.dot(select, fock, preferred_element_type=jnp.float32)
    fock_col = lax.dot_general(
        fock_rows.astype(jnp.bfloat16), select, NT, preferred_element_type=jnp.float32
    )
    diag = jnp.sum(jnp.where(local[:, None] == local[None, :], fock_col, 0.0), axis=1)

    orbs = jnp.concatenate([orb, orb_q, cpl_q.reshape(64, 2)], axis=0)
    at = orbs[:, :, None] == local[None, None, :]
    dsum = jnp.sum(jnp.where(at, diag[None, None, :], 0.0), axis=2)
    dsum = dsum[:, 0] + dsum[:, 1]
    wts = jnp.concatenate([coupling(fock_col, orb, cpl), coupling(fock_col, orb_q, cpl_q)])

    flat = orbs.T.reshape(192)
    offset = (flat // 2) ^ grp
    spot = jnp.stack([found_in(offset, arrival(masks)) for masks in MASKS])
    slot = found_in(cpl_slot.reshape(64) ^ grp, arrival(MASKS[0]))
    return spot * 2 + flat % 2, wts, slot, dsum


def swap(block, mask):
    return lax.ppermute(block, "grp", [(g, g ^ mask) for g in range(16)])


def on_device(
    integrals, metric, fock, virt_energy, send_orb, pair_orb, send_pair, cpl_slot, cpl_orb
):
    orb = pair_orb // 32 * 2 + pair_orb % 2
    cpl = cpl_orb // 32 * 2 + cpl_orb % 2
    metas = jnp.concatenate([orb, cpl.reshape(16, 8)], axis=1).reshape(1, 160)
    metas = jnp.concatenate([metas, send_pair], axis=1)
    for mask in MASKS[0]:
        metas = jnp.concatenate([metas, swap(metas, mask)], axis=0)

    rows = integrals.reshape(64, 16, 512).transpose(1, 0, 2)
    block = lax.all_to_all(rows, "aux", split_axis=0, concat_axis=0, tiled=True)
    block, metas = lax.optimization_barrier((block, metas))
    idx, wts, slot, dsum = tables(metas, fock, orb, cpl, cpl_slot)
    fitted = lax.dot_general(
        block.reshape(1024, 512),
        metric,
        (((0,), (1,)), ((), ())),
        preferred_element_type=jnp.float32,
    ).astype(jnp.bfloat16)
    held = [fitted[None, :, 256 * q : 256 * q + 256] for q in range(4)]
    for step in range(2):
        got = [swap(held[q], MASKS[q][step]) for q in range(4)]
        held = [jnp.concatenate([a, b], axis=0) for a, b in zip(held, got)]
        held = list(lax.optimization_barrier(tuple(held)))
    third = [swap(held[q], MASKS[q][2]) for q in range(4)]
    early = [swap(held[q], MASKS[q][3]) for q in range(4)]
    late = [swap(third[q], MASKS[q][3]) for q in range(4)]
    pieces = [x.reshape(8, 256, 256) for four in zip(held, third, early, late) for x in four]
    return amplitudes(idx, wts, slot, dsum, virt_energy, pieces)


def solution(mesh):
    in_specs = (
        P("aux", "grp", None),
        P(),
        P(),
        P(),
        P(("aux", "grp"), None),
        P(("aux", "grp"), None),
        P(("aux", "grp"), None),
        P(("aux", "grp"), None),
        P(("aux", "grp"), None, None),
    )
    out_specs = P(("aux", "grp"), None, None)
    return jax.shard_map(
        on_device, mesh=mesh, in_specs=in_specs, out_specs=out_specs, check_vma=False
    )
```

```python
import jax
import jax.numpy as jnp
from jax import lax
from jax.experimental import pallas as pl
from jax.experimental.pallas import tpu as pltpu
from jax.sharding import PartitionSpec as P

NT = (((1,), (1,)), ((), ()))
MIB = 2**20
UNROLL = 4
MASKS = ((4, 12, 1, 3), (1, 3, 4, 12), (12, 4, 3, 1), (3, 1, 12, 4))


def recip(x):
    r = pl.reciprocal(x, approx=True)
    return r * (2.0 - x * r)


def listed(wts, order):
    def entry(n, count):
        hit = wts[64 + n] != 0.0

        @pl.when(hit)
        def _():
            order[count] = n

        return count + hit.astype(jnp.int32)

    count = lax.fori_loop(0, 64, entry, 0)
    for k in range(UNROLL):
        order[count + k] = -1
    return (count + UNROLL - 1) // UNROLL


def pair_kernel(idx, wts, slot, dsum, vrow, vcol, *refs):
    pieces, out, pool, mixed, amp, vsum, order, sems, out_sems = refs[:16], *refs[16:]
    copies = [
        pltpu.make_async_copy(
            pieces[4 * q + part], pool.at[q, pl.ds(8 * part, 8)], sems.at[4 * q + part]
        )
        for q in range(4)
        for part in range(4)
    ]
    for copy in copies:
        copy.start()
    trips = listed(wts, order)
    vsum[...] = vrow[...] + vcol[...]

    def clear(s, carry):
        mixed[s] = jnp.zeros((256, 256), jnp.float32)
        return carry

    lax.fori_loop(0, 16, clear, 0)
    for copy in copies:
        copy.wait()

    def product(n):
        left = jnp.concatenate([pool[q, idx[q, n]] for q in range(4)], axis=1)
        right = jnp.concatenate([pool[q, idx[q, 96 + n]] for q in range(4)], axis=1)
        return lax.dot_general(left, right, NT, preferred_element_type=jnp.float32)

    def coupled(g, carry):
        for u in range(UNROLL):
            entry = order[UNROLL * g + u]
            n = jnp.maximum(entry, 0)
            weight = jnp.where(entry >= 0, wts[64 + n], 0.0)
            start = -(product(32 + n) * recip(vsum[...] - dsum[32 + n]))
            rounded = start.astype(jnp.bfloat16).astype(jnp.float32)
            mixed[n // 4] += weight * rounded
        return carry

    def received(g, carry):
        for u in range(UNROLL):
            s = UNROLL * g + u
            value = (mixed[s] - product(16 + s)) * recip(vsum[...] - dsum[16 + s])
            amp[s] = value.astype(jnp.bfloat16)
        return carry

    def out_copy(g):
        rows = pl.ds(UNROLL * g, UNROLL)
        return pltpu.make_async_copy(mixed.at[rows], out.at[rows], out_sems.at[g])

    def own(g, carry):
        for u in range(UNROLL):
            p = UNROLL * g + u
            total = -product(p)
            for e in range(4):
                total += wts[4 * p + e] * amp[slot[4 * p + e]].astype(jnp.float32)
            mixed[p] = total * recip(vsum[...] - dsum[p])
        out_copy(g).start()
        return carry

    def finish(g, carry):
        out_copy(g).wait()
        return carry

    lax.fori_loop(0, trips, coupled, 0)
    lax.fori_loop(0, 16 // UNROLL, received, 0)
    lax.fori_loop(0, 16 // UNROLL, own, 0)
    lax.fori_loop(0, 16 // UNROLL, finish, 0)


SMEM = pl.BlockSpec(memory_space=pltpu.SMEM)
VMEM = pl.BlockSpec(memory_space=pltpu.VMEM)
HBM = pl.BlockSpec(memory_space=pl.ANY)


def amplitudes(idx, wts, slot, dsum, virt, pieces):
    return pl.pallas_call(
        pair_kernel,
        in_specs=[SMEM] * 4 + [VMEM] * 2 + [HBM] * 16,
        out_specs=HBM,
        out_shape=jax.ShapeDtypeStruct((16, 256, 256), jnp.float32),
        scratch_shapes=[
            pltpu.VMEM((4, 32, 256, 256), jnp.bfloat16),
            pltpu.VMEM((16, 256, 256), jnp.float32),
            pltpu.VMEM((16, 256, 256), jnp.bfloat16),
            pltpu.VMEM((256, 256), jnp.float32),
            pltpu.SMEM((72,), jnp.int32),
            pltpu.SemaphoreType.DMA((16,)),
            pltpu.SemaphoreType.DMA((4,)),
        ],
        compiler_params=pltpu.CompilerParams(vmem_limit_bytes=58 * MIB),
        cost_estimate=pl.CostEstimate(
            flops=96 * 2 * 256 * 256 * 1024, bytes_accessed=20 * MIB, transcendentals=0
        ),
    )(idx, wts, slot, dsum, virt[None, :], virt[:, None], *pieces)


def lookup(table, rows, cols):
    ids = jnp.arange(32, dtype=jnp.int32)
    pick = (rows[:, None, None] == ids[None, :, None]) & (
        cols[:, None, None] == ids[None, None, :]
    )
    return jnp.sum(jnp.where(pick, table[None], 0.0), axis=(1, 2))


def coupling(table, orb, cpl):
    i, j = orb[:, 0, None], orb[:, 1, None]
    k, l = cpl[:, :, 0], cpl[:, :, 1]
    first = (l == j) & (k != i)
    second = (k == i) & (l != j)
    rows = jnp.where(first, i, j) + jnp.zeros_like(k)
    cols = jnp.where(first, k, l)
    value = lookup(table, rows.reshape(-1), cols.reshape(-1)).reshape(k.shape)
    return jnp.where(first | second, value, 0.0).reshape(-1)


def arrival(masks):
    order = [0]
    for mask in masks:
        order = order + [o ^ mask for o in order]
    return order


def found_in(values, order):
    ids = jnp.arange(16, dtype=jnp.int32)
    hit = values[..., None] == jnp.array(order, jnp.int32)
    return jnp.sum(jnp.where(hit, ids, 0), axis=-1)


def tables(metas, fock, orb, cpl, cpl_slot):
    col = lax.axis_index("aux")
    grp = lax.axis_index("grp")
    chosen = jnp.sum(
        jnp.where(jnp.arange(16)[None, :] == grp, metas[:, 160:], 0), axis=1
    )
    pick = chosen[:, None, None] == jnp.arange(16, dtype=jnp.int32)[None, :, None]
    sent = jnp.sum(jnp.where(pick, metas[:, :160].reshape(16, 16, 10), 0), axis=1)
    orb_q, cpl_q = sent[:, :2], sent[:, 2:].reshape(16, 4, 2)

    local = jnp.arange(32, dtype=jnp.int32)
    whole = local // 2 * 32 + col * 2 + local % 2
    select = (whole[:, None] == jnp.arange(512)[None, :]).astype(jnp.bfloat16)
    fock_rows = jnp.dot(select, fock, preferred_element_type=jnp.float32)
    fock_col = lax.dot_general(
        fock_rows.astype(jnp.bfloat16), select, NT, preferred_element_type=jnp.float32
    )
    diag = jnp.sum(jnp.where(local[:, None] == local[None, :], fock_col, 0.0), axis=1)

    orbs = jnp.concatenate([orb, orb_q, cpl_q.reshape(64, 2)], axis=0)
    at = orbs[:, :, None] == local[None, None, :]
    dsum = jnp.sum(jnp.where(at, diag[None, None, :], 0.0), axis=2)
    dsum = dsum[:, 0] + dsum[:, 1]
    wts = jnp.concatenate([coupling(fock_col, orb, cpl), coupling(fock_col, orb_q, cpl_q)])

    flat = orbs.T.reshape(192)
    offset = (flat // 2) ^ grp
    spot = jnp.stack([found_in(offset, arrival(masks)) for masks in MASKS])
    slot = found_in(cpl_slot.reshape(64) ^ grp, arrival(MASKS[0]))
    return spot * 2 + flat % 2, wts, slot, dsum


def swap(block, mask):
    return lax.ppermute(block, "grp", [(g, g ^ mask) for g in range(16)])


def join_kernel(*refs):
    held, got, joined = refs[:4], refs[4:8], refs[8:12]
    whole, in_sems, out_sems = refs[12:16], refs[16], refs[17]
    count = held[0].shape[0]

    def in_copies(q):
        return [
            pltpu.make_async_copy(
                source[q], whole[q].at[pl.ds(part * count, count)], in_sems.at[2 * q + part]
            )
            for part, source in enumerate((held, got))
        ]

    copies = [in_copies(q) for q in range(4)]
    outs = [pltpu.make_async_copy(whole[q], joined[q], out_sems.at[q]) for q in range(4)]
    for pair in copies:
        for copy in pair:
            copy.start()
    for pair, out in zip(copies, outs):
        for copy in pair:
            copy.wait()
        out.start()
    for out in outs:
        out.wait()


def join(held, got, grant):
    count, rows, columns = held[0].shape
    shape = (2 * count, rows, columns)
    return pl.pallas_call(
        join_kernel,
        in_specs=[HBM] * 8,
        out_specs=[HBM] * 4,
        out_shape=[jax.ShapeDtypeStruct(shape, jnp.bfloat16)] * 4,
        scratch_shapes=[pltpu.VMEM(shape, jnp.bfloat16)] * 4
        + [pltpu.SemaphoreType.DMA((8,)), pltpu.SemaphoreType.DMA((4,))],
        compiler_params=pltpu.CompilerParams(vmem_limit_bytes=grant * MIB),
        cost_estimate=pl.CostEstimate(
            flops=0, bytes_accessed=16 * count * rows * columns * 2, transcendentals=0
        ),
    )(*held, *got)


def on_device(
    integrals, metric, fock, virt_energy, send_orb, pair_orb, send_pair, cpl_slot, cpl_orb
):
    orb = pair_orb // 32 * 2 + pair_orb % 2
    cpl = cpl_orb // 32 * 2 + cpl_orb % 2
    metas = jnp.concatenate([orb, cpl.reshape(16, 8)], axis=1).reshape(1, 160)
    metas = jnp.concatenate([metas, send_pair], axis=1)
    for mask in MASKS[0]:
        metas = jnp.concatenate([metas, swap(metas, mask)], axis=0)

    rows = integrals.reshape(64, 16, 512).transpose(1, 0, 2)
    block = lax.all_to_all(rows, "aux", split_axis=0, concat_axis=0, tiled=True)
    block, metas = lax.optimization_barrier((block, metas))
    idx, wts, slot, dsum = tables(metas, fock, orb, cpl, cpl_slot)
    fitted = lax.dot_general(
        block.reshape(1024, 512),
        metric,
        (((0,), (1,)), ((), ())),
        preferred_element_type=jnp.float32,
    ).astype(jnp.bfloat16)
    held = [fitted[None, :, 256 * q : 256 * q + 256] for q in range(4)]
    for step in range(2):
        got = [swap(held[q], MASKS[q][step]) for q in range(4)]
        held = join(held, got, (16, 58)[step])
    third = [swap(held[q], MASKS[q][2]) for q in range(4)]
    early = [swap(held[q], MASKS[q][3]) for q in range(4)]
    late = [swap(third[q], MASKS[q][3]) for q in range(4)]
    pieces = [x.reshape(8, 256, 256) for four in zip(held, third, early, late) for x in four]
    return amplitudes(idx, wts, slot, dsum, virt_energy, pieces)


def solution(mesh):
    in_specs = (
        P("aux", "grp", None),
        P(),
        P(),
        P(),
        P(("aux", "grp"), None),
        P(("aux", "grp"), None),
        P(("aux", "grp"), None),
        P(("aux", "grp"), None),
        P(("aux", "grp"), None, None),
    )
    out_specs = P(("aux", "grp"), None, None)
    return jax.shard_map(
        on_device, mesh=mesh, in_specs=in_specs, out_specs=out_specs, check_vma=False
    )
```

```python
import jax
import jax.numpy as jnp
from jax import lax
from jax.experimental import pallas as pl
from jax.experimental.pallas import tpu as pltpu
from jax.sharding import PartitionSpec as P

NT = (((1,), (1,)), ((), ()))
MIB = 2**20
UNROLL = 8
MASKS = ((4, 12, 1, 3), (1, 3, 4, 12), (12, 4, 3, 1), (3, 1, 12, 4))


def recip(x):
    r = pl.reciprocal(x, approx=True)
    return r * (2.0 - x * r)


def listed(idx, wts, order, soon):
    def entry(n, count):
        last = idx[0, 32 + n]
        for q in range(4):
            last = jnp.maximum(last, jnp.maximum(idx[q, 32 + n], idx[q, 128 + n]))
        hit = (wts[64 + n] != 0.0) & ((last < 24) == soon)

        @pl.when(hit)
        def _():
            order[count] = n

        return count + hit.astype(jnp.int32)

    count = lax.fori_loop(0, 64, entry, 0)
    for k in range(UNROLL):
        order[count + k] = -1
    return (count + UNROLL - 1) // UNROLL


def product(idx, pool, n):
    left = jnp.concatenate([pool[q, idx[q, n]] for q in range(4)], axis=1)
    right = jnp.concatenate([pool[q, idx[q, 96 + n]] for q in range(4)], axis=1)
    return lax.dot_general(left, right, NT, preferred_element_type=jnp.float32)


def add_coupled(idx, wts, dsum, pool, mixed, vsum, order, trips):
    def coupled(g, carry):
        for u in range(UNROLL):
            entry = order[UNROLL * g + u]
            n = jnp.maximum(entry, 0)
            weight = jnp.where(entry >= 0, wts[64 + n], 0.0)
            at = jnp.where(entry >= 0, n, order[0])
            start = -(product(idx, pool, 32 + at) * recip(vsum[...] - dsum[32 + at]))
            rounded = start.astype(jnp.bfloat16).astype(jnp.float32)
            mixed[n // 4] += weight * rounded
        return carry

    lax.fori_loop(0, trips, coupled, 0)


def early_kernel(idx, wts, dsum, vrow, vcol, *refs):
    pieces, pool, mixed, vsum, order, sems = refs[:12], *refs[12:]
    copies = [
        pltpu.make_async_copy(
            pieces[3 * q + part], pool.at[q, pl.ds(8 * part, 8)], sems.at[3 * q + part]
        )
        for q in range(4)
        for part in range(3)
    ]
    for copy in copies:
        copy.start()
    trips = listed(idx, wts, order, True)
    vsum[...] = vrow[...] + vcol[...]

    def clear(s, carry):
        mixed[s] = jnp.zeros((256, 256), jnp.float32)
        return carry

    lax.fori_loop(0, 16, clear, 0)
    for copy in copies:
        copy.wait()
    add_coupled(idx, wts, dsum, pool, mixed, vsum, order, trips)


def last_kernel(idx, wts, dsum, vrow, vcol, slot, *refs):
    pieces, _, _, out, pool, mixed, amp, vsum, order, sems, out_sems = refs[:4], *refs[4:]
    copies = [
        pltpu.make_async_copy(pieces[q], pool.at[q, pl.ds(24, 8)], sems.at[q]) for q in range(4)
    ]
    for copy in copies:
        copy.start()
    trips = listed(idx, wts, order, False)
    vsum[...] = vrow[...] + vcol[...]
    for copy in copies:
        copy.wait()
    add_coupled(idx, wts, dsum, pool, mixed, vsum, order, trips)

    def received(g, carry):
        for u in range(UNROLL):
            s = UNROLL * g + u
            value = (mixed[s] - product(idx, pool, 16 + s)) * recip(vsum[...] - dsum[16 + s])
            amp[s] = value.astype(jnp.bfloat16)
        return carry

    def out_copy(g):
        rows = pl.ds(UNROLL * g, UNROLL)
        return pltpu.make_async_copy(mixed.at[rows], out.at[rows], out_sems.at[g])

    def own(g, carry):
        for u in range(UNROLL):
            p = UNROLL * g + u
            total = -product(idx, pool, p)
            for e in range(4):
                total += wts[4 * p + e] * amp[slot[4 * p + e]].astype(jnp.float32)
            mixed[p] = total * recip(vsum[...] - dsum[p])
        out_copy(g).start()
        return carry

    def finish(g, carry):
        out_copy(g).wait()
        return carry

    lax.fori_loop(0, 16 // UNROLL, received, 0)
    lax.fori_loop(0, 16 // UNROLL, own, 0)
    lax.fori_loop(0, 16 // UNROLL, finish, 0)


SMEM = pl.BlockSpec(memory_space=pltpu.SMEM)
VMEM = pl.BlockSpec(memory_space=pltpu.VMEM)
HBM = pl.BlockSpec(memory_space=pl.ANY)


POOL = pltpu.VMEM((4, 32, 256, 256), jnp.bfloat16)
SUMS = pltpu.VMEM((16, 256, 256), jnp.float32)


def early_sums(idx, wts, dsum, vrow, vcol, pieces):
    return pl.pallas_call(
        early_kernel,
        in_specs=[SMEM] * 3 + [VMEM] * 2 + [HBM] * 12,
        out_specs=[VMEM] * 2,
        out_shape=[POOL, SUMS],
        scratch_shapes=[
            pltpu.VMEM((256, 256), jnp.float32),
            pltpu.SMEM((72,), jnp.int32),
            pltpu.SemaphoreType.DMA((12,)),
        ],
        compiler_params=pltpu.CompilerParams(vmem_limit_bytes=36 * MIB),
        cost_estimate=pl.CostEstimate(
            flops=20 * 2 * 256 * 256 * 1024, bytes_accessed=12 * MIB, transcendentals=0
        ),
    )(idx, wts, dsum, vrow, vcol, *pieces)


def amplitudes(idx, wts, dsum, vrow, vcol, slot, pieces, pool, sums):
    return pl.pallas_call(
        last_kernel,
        in_specs=[SMEM] * 3 + [VMEM] * 2 + [SMEM] + [HBM] * 4 + [VMEM] * 2,
        out_specs=[HBM] + [VMEM] * 2,
        out_shape=[jax.ShapeDtypeStruct((16, 256, 256), jnp.float32), POOL, SUMS],
        input_output_aliases={10: 1, 11: 2},
        scratch_shapes=[
            pltpu.VMEM((16, 256, 256), jnp.bfloat16),
            pltpu.VMEM((256, 256), jnp.float32),
            pltpu.SMEM((72,), jnp.int32),
            pltpu.SemaphoreType.DMA((4,)),
            pltpu.SemaphoreType.DMA((4,)),
        ],
        compiler_params=pltpu.CompilerParams(vmem_limit_bytes=8 * MIB),
        cost_estimate=pl.CostEstimate(
            flops=80 * 2 * 256 * 256 * 1024, bytes_accessed=8 * MIB, transcendentals=0
        ),
    )(idx, wts, dsum, vrow, vcol, slot, *pieces, pool, sums)[0]


def lookup(table, rows, cols):
    ids = jnp.arange(32, dtype=jnp.int32)
    pick = (rows[:, None, None] == ids[None, :, None]) & (
        cols[:, None, None] == ids[None, None, :]
    )
    return jnp.sum(jnp.where(pick, table[None], 0.0), axis=(1, 2))


def coupling(table, orb, cpl):
    i, j = orb[:, 0, None], orb[:, 1, None]
    k, l = cpl[:, :, 0], cpl[:, :, 1]
    first = (l == j) & (k != i)
    second = (k == i) & (l != j)
    rows = jnp.where(first, i, j) + jnp.zeros_like(k)
    cols = jnp.where(first, k, l)
    value = lookup(table, rows.reshape(-1), cols.reshape(-1)).reshape(k.shape)
    return jnp.where(first | second, value, 0.0).reshape(-1)


def arrival(masks):
    order = [0]
    for mask in masks:
        order = order + [o ^ mask for o in order]
    return order


def found_in(values, order):
    ids = jnp.arange(16, dtype=jnp.int32)
    hit = values[..., None] == jnp.array(order, jnp.int32)
    return jnp.sum(jnp.where(hit, ids, 0), axis=-1)


def tables(metas, fock, orb, cpl, cpl_slot):
    col = lax.axis_index("aux")
    grp = lax.axis_index("grp")
    chosen = jnp.sum(
        jnp.where(jnp.arange(16)[None, :] == grp, metas[:, 160:], 0), axis=1
    )
    pick = chosen[:, None, None] == jnp.arange(16, dtype=jnp.int32)[None, :, None]
    sent = jnp.sum(jnp.where(pick, metas[:, :160].reshape(16, 16, 10), 0), axis=1)
    orb_q, cpl_q = sent[:, :2], sent[:, 2:].reshape(16, 4, 2)

    local = jnp.arange(32, dtype=jnp.int32)
    whole = local // 2 * 32 + col * 2 + local % 2
    select = (whole[:, None] == jnp.arange(512)[None, :]).astype(jnp.bfloat16)
    fock_rows = jnp.dot(select, fock, preferred_element_type=jnp.float32)
    fock_col = lax.dot_general(
        fock_rows.astype(jnp.bfloat16), select, NT, preferred_element_type=jnp.float32
    )
    diag = jnp.sum(jnp.where(local[:, None] == local[None, :], fock_col, 0.0), axis=1)

    orbs = jnp.concatenate([orb, orb_q, cpl_q.reshape(64, 2)], axis=0)
    at = orbs[:, :, None] == local[None, None, :]
    dsum = jnp.sum(jnp.where(at, diag[None, None, :], 0.0), axis=2)
    dsum = dsum[:, 0] + dsum[:, 1]
    wts = jnp.concatenate([coupling(fock_col, orb, cpl), coupling(fock_col, orb_q, cpl_q)])

    flat = orbs.T.reshape(192)
    offset = (flat // 2) ^ grp
    spot = jnp.stack([found_in(offset, arrival(masks)) for masks in MASKS])
    slot = found_in(cpl_slot.reshape(64) ^ grp, arrival(MASKS[0]))
    return spot * 2 + flat % 2, wts, slot, dsum


def swap(block, mask):
    return lax.ppermute(block, "grp", [(g, g ^ mask) for g in range(16)])


def join_kernel(*refs):
    held, got, joined = refs[:4], refs[4:8], refs[8:12]
    whole, in_sems, out_sems = refs[12:16], refs[16], refs[17]
    count = held[0].shape[0]

    def in_copies(q):
        return [
            pltpu.make_async_copy(
                source[q], whole[q].at[pl.ds(part * count, count)], in_sems.at[2 * q + part]
            )
            for part, source in enumerate((held, got))
        ]

    copies = [in_copies(q) for q in range(4)]
    outs = [pltpu.make_async_copy(whole[q], joined[q], out_sems.at[q]) for q in range(4)]
    for pair in copies:
        for copy in pair:
            copy.start()
    for pair, out in zip(copies, outs):
        for copy in pair:
            copy.wait()
        out.start()
    for out in outs:
        out.wait()


def join(held, got, grant):
    count, rows, columns = held[0].shape
    shape = (2 * count, rows, columns)
    return pl.pallas_call(
        join_kernel,
        in_specs=[HBM] * 8,
        out_specs=[HBM] * 4,
        out_shape=[jax.ShapeDtypeStruct(shape, jnp.bfloat16)] * 4,
        scratch_shapes=[pltpu.VMEM(shape, jnp.bfloat16)] * 4
        + [pltpu.SemaphoreType.DMA((8,)), pltpu.SemaphoreType.DMA((4,))],
        compiler_params=pltpu.CompilerParams(vmem_limit_bytes=grant * MIB),
        cost_estimate=pl.CostEstimate(
            flops=0, bytes_accessed=16 * count * rows * columns * 2, transcendentals=0
        ),
    )(*held, *got)


def on_device(
    integrals, metric, fock, virt_energy, send_orb, pair_orb, send_pair, cpl_slot, cpl_orb
):
    orb = pair_orb // 32 * 2 + pair_orb % 2
    cpl = cpl_orb // 32 * 2 + cpl_orb % 2
    metas = jnp.concatenate([orb, cpl.reshape(16, 8)], axis=1).reshape(1, 160)
    metas = jnp.concatenate([metas, send_pair], axis=1)
    for mask in MASKS[0]:
        metas = jnp.concatenate([metas, swap(metas, mask)], axis=0)

    rows = integrals.reshape(64, 16, 512).transpose(1, 0, 2)
    block = lax.all_to_all(rows, "aux", split_axis=0, concat_axis=0, tiled=True)
    given = (*tables(metas, fock, orb, cpl, cpl_slot), virt_energy[None, :], virt_energy[:, None])
    block, (idx, wts, slot, dsum, vrow, vcol) = lax.optimization_barrier((block, given))
    fitted = lax.dot_general(
        block.reshape(1024, 512),
        metric,
        (((0,), (1,)), ((), ())),
        preferred_element_type=jnp.float32,
    ).astype(jnp.bfloat16)
    held = [fitted[None, :, 256 * q : 256 * q + 256] for q in range(4)]
    for step in range(2):
        got = [swap(held[q], MASKS[q][step]) for q in range(4)]
        held = join(held, got, (16, 58)[step])
    third = [swap(held[q], MASKS[q][2]) for q in range(4)]
    early = [swap(held[q], MASKS[q][3]) for q in range(4)]
    late = [swap(third[q], MASKS[q][3]) for q in range(4)]
    soon = [x.reshape(8, 256, 256) for three in zip(held, third, early) for x in three]
    pool, sums = early_sums(idx, wts, dsum, vrow, vcol, soon)
    late = [x.reshape(8, 256, 256) for x in late]
    return amplitudes(idx, wts, dsum, vrow, vcol, slot, late, pool, sums)


def solution(mesh):
    in_specs = (
        P("aux", "grp", None),
        P(),
        P(),
        P(),
        P(("aux", "grp"), None),
        P(("aux", "grp"), None),
        P(("aux", "grp"), None),
        P(("aux", "grp"), None),
        P(("aux", "grp"), None, None),
    )
    out_specs = P(("aux", "grp"), None, None)
    return jax.shard_map(
        on_device, mesh=mesh, in_specs=in_specs, out_specs=out_specs, check_vma=False
    )
```

```python
import jax
import jax.numpy as jnp
from jax import lax
from jax.experimental import pallas as pl
from jax.experimental.pallas import tpu as pltpu
from jax.sharding import PartitionSpec as P

NT = (((1,), (1,)), ((), ()))
MIB = 2**20
UNROLL = 8
MASKS = ((4, 12, 1, 3), (1, 3, 4, 12), (12, 4, 3, 1), (3, 1, 12, 4))


def recip(x):
    r = pl.reciprocal(x, approx=True)
    return r * (2.0 - x * r)


def listed(idx, wts, order, soon):
    def entry(n, count):
        last = idx[0, 32 + n]
        for q in range(4):
            last = jnp.maximum(last, jnp.maximum(idx[q, 32 + n], idx[q, 128 + n]))
        hit = (wts[64 + n] != 0.0) & ((last < 24) == soon)

        @pl.when(hit)
        def _():
            order[count] = n

        return count + hit.astype(jnp.int32)

    count = lax.fori_loop(0, 64, entry, 0)
    for k in range(UNROLL):
        order[count + k] = -1
    return (count + UNROLL - 1) // UNROLL


def product(idx, pool, n):
    left = jnp.concatenate([pool[q, idx[q, n]] for q in range(4)], axis=1)
    right = jnp.concatenate([pool[q, idx[q, 96 + n]] for q in range(4)], axis=1)
    return lax.dot_general(left, right, NT, preferred_element_type=jnp.float32)


def add_coupled(idx, wts, dsum, pool, mixed, vsum, order, trips):
    def coupled(g, carry):
        for u in range(UNROLL):
            entry = order[UNROLL * g + u]
            n = jnp.maximum(entry, 0)
            weight = jnp.where(entry >= 0, wts[64 + n], 0.0)
            at = jnp.where(entry >= 0, n, order[0])
            start = -(product(idx, pool, 32 + at) * recip(vsum[...] - dsum[32 + at]))
            rounded = start.astype(jnp.bfloat16).astype(jnp.float32)
            mixed[n // 4] += weight * rounded
        return carry

    lax.fori_loop(0, trips, coupled, 0)


def early_kernel(idx, wts, dsum, vrow, vcol, *refs):
    pieces, pool, mixed, vsum, order, sems = refs[:12], *refs[12:]
    copies = [
        pltpu.make_async_copy(
            pieces[3 * q + part], pool.at[q, pl.ds(8 * part, 8)], sems.at[3 * q + part]
        )
        for q in range(4)
        for part in range(3)
    ]
    for copy in copies:
        copy.start()
    trips = listed(idx, wts, order, True)
    vsum[...] = vrow[...] + vcol[...]

    def clear(s, carry):
        mixed[s] = jnp.zeros((256, 256), jnp.float32)
        return carry

    lax.fori_loop(0, 16, clear, 0)
    for copy in copies:
        copy.wait()
    add_coupled(idx, wts, dsum, pool, mixed, vsum, order, trips)


def last_kernel(idx, wts, dsum, vrow, vcol, slot, *refs):
    pieces, _, _, out, pool, mixed, amp, vsum, order, sems, out_sems = refs[:4], *refs[4:]
    copies = [
        pltpu.make_async_copy(pieces[q], pool.at[q, pl.ds(24, 8)], sems.at[q]) for q in range(4)
    ]
    for copy in copies:
        copy.start()
    trips = listed(idx, wts, order, False)
    vsum[...] = vrow[...] + vcol[...]
    for copy in copies:
        copy.wait()
    add_coupled(idx, wts, dsum, pool, mixed, vsum, order, trips)

    def received(g, carry):
        for u in range(UNROLL):
            s = UNROLL * g + u
            value = (mixed[s] - product(idx, pool, 16 + s)) * recip(vsum[...] - dsum[16 + s])
            amp[s] = value.astype(jnp.bfloat16)
        return carry

    def out_copy(g):
        rows = pl.ds(UNROLL * g, UNROLL)
        return pltpu.make_async_copy(mixed.at[rows], out.at[rows], out_sems.at[g])

    def own(g, carry):
        for u in range(UNROLL):
            p = UNROLL * g + u
            total = -product(idx, pool, p)
            for e in range(4):
                total += wts[4 * p + e] * amp[slot[4 * p + e]].astype(jnp.float32)
            mixed[p] = total * recip(vsum[...] - dsum[p])
        out_copy(g).start()
        return carry

    def finish(g, carry):
        out_copy(g).wait()
        return carry

    lax.fori_loop(0, 16 // UNROLL, received, 0)
    lax.fori_loop(0, 16 // UNROLL, own, 0)
    lax.fori_loop(0, 16 // UNROLL, finish, 0)


SMEM = pl.BlockSpec(memory_space=pltpu.SMEM)
VMEM = pl.BlockSpec(memory_space=pltpu.VMEM)
HBM = pl.BlockSpec(memory_space=pl.ANY)


POOL = pltpu.VMEM((4, 32, 256, 256), jnp.bfloat16)
SUMS = pltpu.VMEM((16, 256, 256), jnp.float32)


def early_sums(idx, wts, dsum, vrow, vcol, pieces):
    return pl.pallas_call(
        early_kernel,
        in_specs=[SMEM] * 3 + [VMEM] * 2 + [HBM] * 12,
        out_specs=[VMEM] * 2,
        out_shape=[POOL, SUMS],
        scratch_shapes=[
            pltpu.VMEM((256, 256), jnp.float32),
            pltpu.SMEM((72,), jnp.int32),
            pltpu.SemaphoreType.DMA((12,)),
        ],
        compiler_params=pltpu.CompilerParams(vmem_limit_bytes=36 * MIB),
        cost_estimate=pl.CostEstimate(
            flops=20 * 2 * 256 * 256 * 1024, bytes_accessed=12 * MIB, transcendentals=0
        ),
    )(idx, wts, dsum, vrow, vcol, *pieces)


def amplitudes(idx, wts, dsum, vrow, vcol, slot, pieces, pool, sums):
    return pl.pallas_call(
        last_kernel,
        in_specs=[SMEM] * 3 + [VMEM] * 2 + [SMEM] + [HBM] * 4 + [VMEM] * 2,
        out_specs=[HBM] + [VMEM] * 2,
        out_shape=[jax.ShapeDtypeStruct((16, 256, 256), jnp.float32), POOL, SUMS],
        input_output_aliases={10: 1, 11: 2},
        scratch_shapes=[
            pltpu.VMEM((16, 256, 256), jnp.bfloat16),
            pltpu.VMEM((256, 256), jnp.float32),
            pltpu.SMEM((72,), jnp.int32),
            pltpu.SemaphoreType.DMA((4,)),
            pltpu.SemaphoreType.DMA((4,)),
        ],
        compiler_params=pltpu.CompilerParams(vmem_limit_bytes=8 * MIB),
        cost_estimate=pl.CostEstimate(
            flops=80 * 2 * 256 * 256 * 1024, bytes_accessed=8 * MIB, transcendentals=0
        ),
    )(idx, wts, dsum, vrow, vcol, slot, *pieces, pool, sums)[0]


def lookup(table, rows, cols):
    ids = jnp.arange(32, dtype=jnp.int32)
    pick = (rows[:, None, None] == ids[None, :, None]) & (
        cols[:, None, None] == ids[None, None, :]
    )
    return jnp.sum(jnp.where(pick, table[None], 0.0), axis=(1, 2))


def coupling(table, orb, cpl):
    i, j = orb[:, 0, None], orb[:, 1, None]
    k, l = cpl[:, :, 0], cpl[:, :, 1]
    first = (l == j) & (k != i)
    second = (k == i) & (l != j)
    rows = jnp.where(first, i, j) + jnp.zeros_like(k)
    cols = jnp.where(first, k, l)
    value = lookup(table, rows.reshape(-1), cols.reshape(-1)).reshape(k.shape)
    return jnp.where(first | second, value, 0.0).reshape(-1)


def arrival(masks):
    order = [0]
    for mask in masks:
        order = order + [o ^ mask for o in order]
    return order


def found_in(values, order):
    ids = jnp.arange(16, dtype=jnp.int32)
    hit = values[..., None] == jnp.array(order, jnp.int32)
    return jnp.sum(jnp.where(hit, ids, 0), axis=-1)


def tables(metas, fock, orb, cpl, cpl_slot):
    col = lax.axis_index("aux")
    grp = lax.axis_index("grp")
    chosen = jnp.sum(
        jnp.where(jnp.arange(16)[None, :] == grp, metas[:, 160:], 0), axis=1
    )
    pick = chosen[:, None, None] == jnp.arange(16, dtype=jnp.int32)[None, :, None]
    sent = jnp.sum(jnp.where(pick, metas[:, :160].reshape(16, 16, 10), 0), axis=1)
    orb_q, cpl_q = sent[:, :2], sent[:, 2:].reshape(16, 4, 2)

    local = jnp.arange(32, dtype=jnp.int32)
    whole = local // 2 * 32 + col * 2 + local % 2
    select = (whole[:, None] == jnp.arange(512)[None, :]).astype(jnp.bfloat16)
    fock_rows = jnp.dot(select, fock, preferred_element_type=jnp.float32)
    fock_col = lax.dot_general(
        fock_rows.astype(jnp.bfloat16), select, NT, preferred_element_type=jnp.float32
    )
    diag = jnp.sum(jnp.where(local[:, None] == local[None, :], fock_col, 0.0), axis=1)

    orbs = jnp.concatenate([orb, orb_q, cpl_q.reshape(64, 2)], axis=0)
    at = orbs[:, :, None] == local[None, None, :]
    dsum = jnp.sum(jnp.where(at, diag[None, None, :], 0.0), axis=2)
    dsum = dsum[:, 0] + dsum[:, 1]
    wts = jnp.concatenate([coupling(fock_col, orb, cpl), coupling(fock_col, orb_q, cpl_q)])

    flat = orbs.T.reshape(192)
    offset = (flat // 2) ^ grp
    spot = jnp.stack([found_in(offset, arrival(masks)) for masks in MASKS])
    slot = found_in(cpl_slot.reshape(64) ^ grp, arrival(MASKS[0]))
    return spot * 2 + flat % 2, wts, slot, dsum


def swap(block, mask):
    return lax.ppermute(block, "grp", [(g, g ^ mask) for g in range(16)])


def join_kernel(*refs):
    held, got, joined = refs[:4], refs[4:8], refs[8:12]
    whole, in_sems, out_sems = refs[12:16], refs[16], refs[17]
    count = held[0].shape[0]

    def in_copies(q):
        return [
            pltpu.make_async_copy(
                source[q], whole[q].at[pl.ds(part * count, count)], in_sems.at[2 * q + part]
            )
            for part, source in enumerate((held, got))
        ]

    copies = [in_copies(q) for q in range(4)]
    outs = [pltpu.make_async_copy(whole[q], joined[q], out_sems.at[q]) for q in range(4)]
    for pair in copies:
        for copy in pair:
            copy.start()
    for pair, out in zip(copies, outs):
        for copy in pair:
            copy.wait()
        out.start()
    for out in outs:
        out.wait()


def join(held, got, grant):
    count, rows, columns = held[0].shape
    shape = (2 * count, rows, columns)
    return pl.pallas_call(
        join_kernel,
        in_specs=[HBM] * 8,
        out_specs=[HBM] * 4,
        out_shape=[jax.ShapeDtypeStruct(shape, jnp.bfloat16)] * 4,
        scratch_shapes=[pltpu.VMEM(shape, jnp.bfloat16)] * 4
        + [pltpu.SemaphoreType.DMA((8,)), pltpu.SemaphoreType.DMA((4,))],
        compiler_params=pltpu.CompilerParams(vmem_limit_bytes=grant * MIB),
        cost_estimate=pl.CostEstimate(
            flops=0, bytes_accessed=16 * count * rows * columns * 2, transcendentals=0
        ),
    )(*held, *got)


def on_device(
    integrals, metric, fock, virt_energy, send_orb, pair_orb, send_pair, cpl_slot, cpl_orb
):
    rows = integrals.reshape(64, 16, 512).transpose(1, 0, 2)
    rows, pair_orb, cpl_orb, send_pair = lax.optimization_barrier(
        (rows, pair_orb, cpl_orb, send_pair)
    )
    orb = pair_orb // 32 * 2 + pair_orb % 2
    cpl = cpl_orb // 32 * 2 + cpl_orb % 2
    metas = jnp.concatenate([orb, cpl.reshape(16, 8)], axis=1).reshape(1, 160)
    metas = jnp.concatenate([metas, send_pair], axis=1)
    for mask in MASKS[0]:
        metas = jnp.concatenate([metas, swap(metas, mask)], axis=0)

    block = lax.all_to_all(rows, "aux", split_axis=0, concat_axis=0, tiled=True)
    given = (*tables(metas, fock, orb, cpl, cpl_slot), virt_energy[None, :], virt_energy[:, None])
    block, (idx, wts, slot, dsum, vrow, vcol) = lax.optimization_barrier((block, given))
    fitted = lax.dot_general(
        block.reshape(1024, 512),
        metric,
        (((0,), (1,)), ((), ())),
        preferred_element_type=jnp.float32,
    ).astype(jnp.bfloat16)
    held = [fitted[None, :, 256 * q : 256 * q + 256] for q in range(4)]
    for step in range(2):
        got = [swap(held[q], MASKS[q][step]) for q in range(4)]
        held = join(held, got, (16, 58)[step])
    third = [swap(held[q], MASKS[q][2]) for q in range(4)]
    early = [swap(held[q], MASKS[q][3]) for q in range(4)]
    late = [swap(third[q], MASKS[q][3]) for q in range(4)]
    soon = [x.reshape(8, 256, 256) for three in zip(held, third, early) for x in three]
    pool, sums = early_sums(idx, wts, dsum, vrow, vcol, soon)
    late = [x.reshape(8, 256, 256) for x in late]
    return amplitudes(idx, wts, dsum, vrow, vcol, slot, late, pool, sums)


def solution(mesh):
    in_specs = (
        P("aux", "grp", None),
        P(),
        P(),
        P(),
        P(("aux", "grp"), None),
        P(("aux", "grp"), None),
        P(("aux", "grp"), None),
        P(("aux", "grp"), None),
        P(("aux", "grp"), None, None),
    )
    out_specs = P(("aux", "grp"), None, None)
    return jax.shard_map(
        on_device, mesh=mesh, in_specs=in_specs, out_specs=out_specs, check_vma=False
    )
```

```python
import jax
import jax.numpy as jnp
from jax import lax
from jax.experimental import pallas as pl
from jax.experimental.pallas import tpu as pltpu
from jax.sharding import PartitionSpec as P

NT = (((1,), (1,)), ((), ()))
MIB = 2**20
UNROLL = 8
MASKS = ((4, 12, 1, 3), (1, 3, 4, 12), (12, 4, 3, 1), (3, 1, 12, 4))


def recip(x):
    r = pl.reciprocal(x, approx=True)
    return r * (2.0 - x * r)


def listed(idx, twin, order, soon):
    def entry(n, count):
        last = idx[0, 32 + n]
        for q in range(4):
            last = jnp.maximum(last, jnp.maximum(idx[q, 32 + n], idx[q, 128 + n]))
        hit = (twin[n] >= -1) & ((last < 24) == soon)

        @pl.when(hit)
        def _():
            order[count] = n

        return count + hit.astype(jnp.int32)

    count = lax.fori_loop(0, 64, entry, 0)
    for k in range(UNROLL):
        order[count + k] = -1
    return (count + UNROLL - 1) // UNROLL


def product(idx, pool, n):
    left = jnp.concatenate([pool[q, idx[q, n]] for q in range(4)], axis=1)
    right = jnp.concatenate([pool[q, idx[q, 96 + n]] for q in range(4)], axis=1)
    return lax.dot_general(left, right, NT, preferred_element_type=jnp.float32)


def add_coupled(idx, wts, twin, dsum, pool, mixed, vsum, order, trips):
    def coupled(g, carry):
        for u in range(UNROLL):
            entry = order[UNROLL * g + u]
            n = jnp.maximum(entry, 0)
            weight = jnp.where(entry >= 0, wts[64 + n], 0.0)
            at = jnp.where(entry >= 0, n, order[0])
            start = -(product(idx, pool, 32 + at) * recip(vsum[...] - dsum[32 + at]))
            rounded = start.astype(jnp.bfloat16).astype(jnp.float32)
            mixed[n // 4] += weight * rounded
            other = jnp.where(entry >= 0, twin[n], -1)
            m = jnp.maximum(other, 0)
            mixed[m // 4] += jnp.where(other >= 0, wts[64 + m], 0.0) * rounded
        return carry

    lax.fori_loop(0, trips, coupled, 0)


def early_kernel(idx, wts, twin, dsum, vrow, vcol, *refs):
    pieces, pool, mixed, vsum, order, sems = refs[:12], *refs[12:]
    copies = [
        pltpu.make_async_copy(
            pieces[3 * q + part], pool.at[q, pl.ds(8 * part, 8)], sems.at[3 * q + part]
        )
        for q in range(4)
        for part in range(3)
    ]
    for copy in copies:
        copy.start()
    trips = listed(idx, twin, order, True)
    vsum[...] = vrow[...] + vcol[...]

    def clear(s, carry):
        mixed[s] = jnp.zeros((256, 256), jnp.float32)
        return carry

    lax.fori_loop(0, 16, clear, 0)
    for copy in copies:
        copy.wait()
    add_coupled(idx, wts, twin, dsum, pool, mixed, vsum, order, trips)


def last_kernel(idx, wts, twin, dsum, vrow, vcol, slot, *refs):
    pieces, _, _, out, pool, mixed, amp, vsum, order, sems, out_sems = refs[:4], *refs[4:]
    copies = [
        pltpu.make_async_copy(pieces[q], pool.at[q, pl.ds(24, 8)], sems.at[q]) for q in range(4)
    ]
    for copy in copies:
        copy.start()
    trips = listed(idx, twin, order, False)
    vsum[...] = vrow[...] + vcol[...]
    for copy in copies:
        copy.wait()
    add_coupled(idx, wts, twin, dsum, pool, mixed, vsum, order, trips)

    def received(g, carry):
        for u in range(UNROLL):
            s = UNROLL * g + u
            value = (mixed[s] - product(idx, pool, 16 + s)) * recip(vsum[...] - dsum[16 + s])
            amp[s] = value.astype(jnp.bfloat16)
        return carry

    def out_copy(p):
        return pltpu.make_async_copy(mixed.at[p], out.at[p], out_sems.at[p])

    def own(g, carry):
        for u in range(UNROLL):
            p = UNROLL * g + u
            total = -product(idx, pool, p)
            for e in range(4):
                total += wts[4 * p + e] * amp[slot[4 * p + e]].astype(jnp.float32)
            mixed[p] = total * recip(vsum[...] - dsum[p])
            out_copy(p).start()
        return carry

    def finish(p, carry):
        out_copy(p).wait()
        return carry

    lax.fori_loop(0, 16 // UNROLL, received, 0)
    lax.fori_loop(0, 16 // UNROLL, own, 0)
    lax.fori_loop(0, 16, finish, 0)


SMEM = pl.BlockSpec(memory_space=pltpu.SMEM)
VMEM = pl.BlockSpec(memory_space=pltpu.VMEM)
HBM = pl.BlockSpec(memory_space=pl.ANY)


POOL = pltpu.VMEM((4, 32, 256, 256), jnp.bfloat16)
SUMS = pltpu.VMEM((16, 256, 256), jnp.float32)


def early_sums(idx, wts, twin, dsum, vrow, vcol, pieces):
    return pl.pallas_call(
        early_kernel,
        in_specs=[SMEM] * 4 + [VMEM] * 2 + [HBM] * 12,
        out_specs=[VMEM] * 2,
        out_shape=[POOL, SUMS],
        scratch_shapes=[
            pltpu.VMEM((256, 256), jnp.float32),
            pltpu.SMEM((72,), jnp.int32),
            pltpu.SemaphoreType.DMA((12,)),
        ],
        compiler_params=pltpu.CompilerParams(vmem_limit_bytes=36 * MIB),
        cost_estimate=pl.CostEstimate(
            flops=20 * 2 * 256 * 256 * 1024, bytes_accessed=12 * MIB, transcendentals=0
        ),
    )(idx, wts, twin, dsum, vrow, vcol, *pieces)


def amplitudes(idx, wts, twin, dsum, vrow, vcol, slot, pieces, pool, sums):
    return pl.pallas_call(
        last_kernel,
        in_specs=[SMEM] * 4 + [VMEM] * 2 + [SMEM] + [HBM] * 4 + [VMEM] * 2,
        out_specs=[HBM] + [VMEM] * 2,
        out_shape=[jax.ShapeDtypeStruct((16, 256, 256), jnp.float32), POOL, SUMS],
        input_output_aliases={11: 1, 12: 2},
        scratch_shapes=[
            pltpu.VMEM((16, 256, 256), jnp.bfloat16),
            pltpu.VMEM((256, 256), jnp.float32),
            pltpu.SMEM((72,), jnp.int32),
            pltpu.SemaphoreType.DMA((4,)),
            pltpu.SemaphoreType.DMA((16,)),
        ],
        compiler_params=pltpu.CompilerParams(vmem_limit_bytes=8 * MIB),
        cost_estimate=pl.CostEstimate(
            flops=80 * 2 * 256 * 256 * 1024, bytes_accessed=8 * MIB, transcendentals=0
        ),
    )(idx, wts, twin, dsum, vrow, vcol, slot, *pieces, pool, sums)[0]


def lookup(table, rows, cols):
    ids = jnp.arange(32, dtype=jnp.int32)
    pick = (rows[:, None, None] == ids[None, :, None]) & (
        cols[:, None, None] == ids[None, None, :]
    )
    return jnp.sum(jnp.where(pick, table[None], 0.0), axis=(1, 2))


def coupling(table, orb, cpl):
    i, j = orb[:, 0, None], orb[:, 1, None]
    k, l = cpl[:, :, 0], cpl[:, :, 1]
    first = (l == j) & (k != i)
    second = (k == i) & (l != j)
    rows = jnp.where(first, i, j) + jnp.zeros_like(k)
    cols = jnp.where(first, k, l)
    value = lookup(table, rows.reshape(-1), cols.reshape(-1)).reshape(k.shape)
    return jnp.where(first | second, value, 0.0).reshape(-1)


def arrival(masks):
    order = [0]
    for mask in masks:
        order = order + [o ^ mask for o in order]
    return order


def found_in(values, order):
    ids = jnp.arange(16, dtype=jnp.int32)
    hit = values[..., None] == jnp.array(order, jnp.int32)
    return jnp.sum(jnp.where(hit, ids, 0), axis=-1)


def twins(pairs, wts):
    n = jnp.arange(64, dtype=jnp.int32)
    code = jnp.where(wts != 0.0, pairs[:, 0] * 32 + pairs[:, 1], -1 - n)
    same = code[:, None] == code[None, :]
    rank = jnp.sum((same & (n[None, :] < n[:, None])).astype(jnp.int32), axis=1)
    after = same & (rank[None, :] == rank[:, None] + 1)
    second = jnp.max(jnp.where(after, n[None, :], -1), axis=1)
    return jnp.where((wts != 0.0) & (rank % 2 == 0), second, -2)


def tables(metas, fock, orb, cpl, cpl_slot):
    col = lax.axis_index("aux")
    grp = lax.axis_index("grp")
    chosen = jnp.sum(
        jnp.where(jnp.arange(16)[None, :] == grp, metas[:, 160:], 0), axis=1
    )
    pick = chosen[:, None, None] == jnp.arange(16, dtype=jnp.int32)[None, :, None]
    sent = jnp.sum(jnp.where(pick, metas[:, :160].reshape(16, 16, 10), 0), axis=1)
    orb_q, cpl_q = sent[:, :2], sent[:, 2:].reshape(16, 4, 2)

    local = jnp.arange(32, dtype=jnp.int32)
    whole = local // 2 * 32 + col * 2 + local % 2
    select = (whole[:, None] == jnp.arange(512)[None, :]).astype(jnp.bfloat16)
    fock_rows = jnp.dot(select, fock, preferred_element_type=jnp.float32)
    fock_col = lax.dot_general(
        fock_rows.astype(jnp.bfloat16), select, NT, preferred_element_type=jnp.float32
    )
    diag = jnp.sum(jnp.where(local[:, None] == local[None, :], fock_col, 0.0), axis=1)

    orbs = jnp.concatenate([orb, orb_q, cpl_q.reshape(64, 2)], axis=0)
    at = orbs[:, :, None] == local[None, None, :]
    dsum = jnp.sum(jnp.where(at, diag[None, None, :], 0.0), axis=2)
    dsum = dsum[:, 0] + dsum[:, 1]
    wts = jnp.concatenate([coupling(fock_col, orb, cpl), coupling(fock_col, orb_q, cpl_q)])

    flat = orbs.T.reshape(192)
    offset = (flat // 2) ^ grp
    spot = jnp.stack([found_in(offset, arrival(masks)) for masks in MASKS])
    slot = found_in(cpl_slot.reshape(64) ^ grp, arrival(MASKS[0]))
    return spot * 2 + flat % 2, wts, twins(cpl_q.reshape(64, 2), wts[64:]), slot, dsum


def swap(block, mask):
    return lax.ppermute(block, "grp", [(g, g ^ mask) for g in range(16)])


def join_kernel(*refs):
    held, got, joined = refs[:4], refs[4:8], refs[8:12]
    whole, in_sems, out_sems = refs[12:16], refs[16], refs[17]
    count = held[0].shape[0]

    def in_copies(q):
        return [
            pltpu.make_async_copy(
                source[q], whole[q].at[pl.ds(part * count, count)], in_sems.at[2 * q + part]
            )
            for part, source in enumerate((held, got))
        ]

    copies = [in_copies(q) for q in range(4)]
    outs = [pltpu.make_async_copy(whole[q], joined[q], out_sems.at[q]) for q in range(4)]
    for pair in copies:
        for copy in pair:
            copy.start()
    for pair, out in zip(copies, outs):
        for copy in pair:
            copy.wait()
        out.start()
    for out in outs:
        out.wait()


def join(held, got, grant):
    count, rows, columns = held[0].shape
    shape = (2 * count, rows, columns)
    return pl.pallas_call(
        join_kernel,
        in_specs=[HBM] * 8,
        out_specs=[HBM] * 4,
        out_shape=[jax.ShapeDtypeStruct(shape, jnp.bfloat16)] * 4,
        scratch_shapes=[pltpu.VMEM(shape, jnp.bfloat16)] * 4
        + [pltpu.SemaphoreType.DMA((8,)), pltpu.SemaphoreType.DMA((4,))],
        compiler_params=pltpu.CompilerParams(vmem_limit_bytes=grant * MIB),
        cost_estimate=pl.CostEstimate(
            flops=0, bytes_accessed=16 * count * rows * columns * 2, transcendentals=0
        ),
    )(*held, *got)


def stage_kernel(*refs):
    held, staged = refs[:4], refs[4:8]
    part, in_sems, out_sems = refs[8:12], refs[12], refs[13]
    ins = [pltpu.make_async_copy(held[q], part[q], in_sems.at[q]) for q in range(4)]
    outs = [
        pltpu.make_async_copy(part[q], staged[q].at[pl.ds(0, 2)], out_sems.at[q]) for q in range(4)
    ]
    for copy in ins:
        copy.start()
    for copy, out in zip(ins, outs):
        copy.wait()
        out.start()
    for out in outs:
        out.wait()


def fill_kernel(*refs):
    got, whole = refs[:4], refs[8:12]
    part, in_sems, out_sems = refs[12:16], refs[16], refs[17]
    ins = [pltpu.make_async_copy(got[q], part[q], in_sems.at[q]) for q in range(4)]
    outs = [
        pltpu.make_async_copy(part[q], whole[q].at[pl.ds(2, 2)], out_sems.at[q]) for q in range(4)
    ]
    for copy in ins:
        copy.start()
    for copy, out in zip(ins, outs):
        copy.wait()
        out.start()
    for out in outs:
        out.wait()


def half_call(kernel, blocks, staged):
    shape = (4, *blocks[0].shape[1:])
    return pl.pallas_call(
        kernel,
        in_specs=[HBM] * (4 + len(staged)),
        out_specs=[HBM] * 4,
        out_shape=[jax.ShapeDtypeStruct(shape, jnp.bfloat16)] * 4,
        input_output_aliases={4 + q: q for q in range(len(staged))},
        scratch_shapes=[pltpu.VMEM(blocks[0].shape, jnp.bfloat16)] * 4
        + [pltpu.SemaphoreType.DMA((4,)), pltpu.SemaphoreType.DMA((4,))],
        compiler_params=pltpu.CompilerParams(vmem_limit_bytes=58 * MIB),
        cost_estimate=pl.CostEstimate(flops=0, bytes_accessed=4 * MIB, transcendentals=0),
    )(*blocks, *staged)


def on_device(
    integrals, metric, fock, virt_energy, send_orb, pair_orb, send_pair, cpl_slot, cpl_orb
):
    rows = integrals.reshape(64, 16, 512).transpose(1, 0, 2)
    rows, pair_orb, cpl_orb, send_pair = lax.optimization_barrier(
        (rows, pair_orb, cpl_orb, send_pair)
    )
    orb = pair_orb // 32 * 2 + pair_orb % 2
    cpl = cpl_orb // 32 * 2 + cpl_orb % 2
    metas = jnp.concatenate([orb, cpl.reshape(16, 8)], axis=1).reshape(1, 160)
    metas = jnp.concatenate([metas, send_pair], axis=1)
    for mask in MASKS[0]:
        metas = jnp.concatenate([metas, swap(metas, mask)], axis=0)

    block = lax.all_to_all(rows, "aux", split_axis=0, concat_axis=0, tiled=True)
    given = (*tables(metas, fock, orb, cpl, cpl_slot), virt_energy[None, :], virt_energy[:, None])
    block, (idx, wts, twin, slot, dsum, vrow, vcol) = lax.optimization_barrier((block, given))
    fitted = lax.dot_general(
        block.reshape(1024, 512),
        metric,
        (((0,), (1,)), ((), ())),
        preferred_element_type=jnp.float32,
    ).astype(jnp.bfloat16)
    held = [fitted[None, :, 256 * q : 256 * q + 256] for q in range(4)]
    got = [swap(held[q], MASKS[q][0]) for q in range(4)]
    held = join(held, got, 16)
    got = [swap(held[q], MASKS[q][1]) for q in range(4)]
    held = half_call(fill_kernel, got, half_call(stage_kernel, held, []))
    third = [swap(held[q], MASKS[q][2]) for q in range(4)]
    early = [swap(held[q], MASKS[q][3]) for q in range(4)]
    late = [swap(third[q], MASKS[q][3]) for q in range(4)]
    soon = [x.reshape(8, 256, 256) for three in zip(held, third, early) for x in three]
    pool, sums = early_sums(idx, wts, twin, dsum, vrow, vcol, soon)
    late = [x.reshape(8, 256, 256) for x in late]
    return amplitudes(idx, wts, twin, dsum, vrow, vcol, slot, late, pool, sums)


def solution(mesh):
    in_specs = (
        P("aux", "grp", None),
        P(),
        P(),
        P(),
        P(("aux", "grp"), None),
        P(("aux", "grp"), None),
        P(("aux", "grp"), None),
        P(("aux", "grp"), None),
        P(("aux", "grp"), None, None),
    )
    out_specs = P(("aux", "grp"), None, None)
    return jax.shard_map(
        on_device, mesh=mesh, in_specs=in_specs, out_specs=out_specs, check_vma=False
    )
```

```python
import jax
import jax.numpy as jnp
from jax import lax
from jax.experimental import pallas as pl
from jax.experimental.pallas import tpu as pltpu
from jax.sharding import PartitionSpec as P

NT = (((1,), (1,)), ((), ()))
MIB = 2**20
UNROLL = 8
MASKS = ((4, 12, 1, 3), (1, 3, 4, 12), (12, 4, 3, 1), (3, 1, 12, 4))


def recip(x):
    r = pl.reciprocal(x, approx=True)
    return r * (2.0 - x * r)


def listed(when, kernel, order):
    def entry(n, count):
        hit = when[n] == kernel

        @pl.when(hit)
        def _():
            order[count] = n

        return count + hit.astype(jnp.int32)

    count = lax.fori_loop(0, 64, entry, 0)
    for k in range(UNROLL):
        order[count + k] = -1
    return (count + UNROLL - 1) // UNROLL


def product(idx, pool, n):
    left = jnp.concatenate([pool[q, idx[q, n]] for q in range(4)], axis=1)
    right = jnp.concatenate([pool[q, idx[q, 96 + n]] for q in range(4)], axis=1)
    return lax.dot_general(left, right, NT, preferred_element_type=jnp.float32)


def add_coupled(idx, wts, dsum, pool, mixed, vsum, order, trips):
    def coupled(g, carry):
        for u in range(UNROLL):
            entry = order[UNROLL * g + u]
            n = jnp.maximum(entry, 0)
            weight = jnp.where(entry >= 0, wts[64 + n], 0.0)
            at = jnp.where(entry >= 0, n, order[0])
            start = -(product(idx, pool, 32 + at) * recip(vsum[...] - dsum[32 + at]))
            rounded = start.astype(jnp.bfloat16).astype(jnp.float32)
            mixed[n // 4] += weight * rounded
        return carry

    lax.fori_loop(0, trips, coupled, 0)


def early_kernel(idx, wts, when, dsum, vrow, vcol, *refs):
    pieces, pool, mixed, vsum, order, sems = refs[:12], *refs[12:]
    copies = [
        pltpu.make_async_copy(
            pieces[3 * q + part], pool.at[q, pl.ds(8 * part, 8)], sems.at[3 * q + part]
        )
        for q in range(4)
        for part in range(3)
    ]
    for copy in copies:
        copy.start()
    trips = listed(when, 1, order)
    vsum[...] = vrow[...] + vcol[...]

    def clear(s, carry):
        mixed[s] = jnp.zeros((256, 256), jnp.float32)
        return carry

    lax.fori_loop(0, 16, clear, 0)
    for copy in copies:
        copy.wait()
    add_coupled(idx, wts, dsum, pool, mixed, vsum, order, trips)


def last_kernel(idx, wts, when, dsum, vrow, vcol, slot, *refs):
    pieces, _, _, out, pool, mixed, amp, vsum, order, sems, out_sems = refs[:4], *refs[4:]
    copies = [
        pltpu.make_async_copy(pieces[q], pool.at[q, pl.ds(24, 8)], sems.at[q]) for q in range(4)
    ]
    for copy in copies:
        copy.start()
    trips = listed(when, 2, order)
    vsum[...] = vrow[...] + vcol[...]
    for copy in copies:
        copy.wait()
    add_coupled(idx, wts, dsum, pool, mixed, vsum, order, trips)

    def received(g, carry):
        for u in range(UNROLL):
            s = UNROLL * g + u
            value = (mixed[s] - product(idx, pool, 16 + s)) * recip(vsum[...] - dsum[16 + s])
            amp[s] = value.astype(jnp.bfloat16)
        return carry

    def out_copy(g):
        rows = pl.ds(UNROLL * g, UNROLL)
        return pltpu.make_async_copy(mixed.at[rows], out.at[rows], out_sems.at[g])

    def own(g, carry):
        for u in range(UNROLL):
            p = UNROLL * g + u
            total = -product(idx, pool, p)
            for e in range(4):
                total += wts[4 * p + e] * amp[slot[4 * p + e]].astype(jnp.float32)
            mixed[p] = total * recip(vsum[...] - dsum[p])
        out_copy(g).start()
        return carry

    def finish(g, carry):
        out_copy(g).wait()
        return carry

    lax.fori_loop(0, 16 // UNROLL, received, 0)
    lax.fori_loop(0, 16 // UNROLL, own, 0)
    lax.fori_loop(0, 16 // UNROLL, finish, 0)


SMEM = pl.BlockSpec(memory_space=pltpu.SMEM)
VMEM = pl.BlockSpec(memory_space=pltpu.VMEM)
HBM = pl.BlockSpec(memory_space=pl.ANY)


POOL = pltpu.VMEM((4, 32, 256, 256), jnp.bfloat16)
SUMS = pltpu.VMEM((16, 256, 256), jnp.float32)


def early_sums(idx, wts, when, dsum, vrow, vcol, pieces):
    return pl.pallas_call(
        early_kernel,
        in_specs=[SMEM] * 4 + [VMEM] * 2 + [HBM] * 12,
        out_specs=[VMEM] * 2,
        out_shape=[POOL, SUMS],
        scratch_shapes=[
            pltpu.VMEM((256, 256), jnp.float32),
            pltpu.SMEM((72,), jnp.int32),
            pltpu.SemaphoreType.DMA((12,)),
        ],
        compiler_params=pltpu.CompilerParams(vmem_limit_bytes=36 * MIB),
        cost_estimate=pl.CostEstimate(
            flops=20 * 2 * 256 * 256 * 1024, bytes_accessed=12 * MIB, transcendentals=0
        ),
    )(idx, wts, when, dsum, vrow, vcol, *pieces)


def amplitudes(idx, wts, when, dsum, vrow, vcol, slot, pieces, pool, sums):
    return pl.pallas_call(
        last_kernel,
        in_specs=[SMEM] * 4 + [VMEM] * 2 + [SMEM] + [HBM] * 4 + [VMEM] * 2,
        out_specs=[HBM] + [VMEM] * 2,
        out_shape=[jax.ShapeDtypeStruct((16, 256, 256), jnp.float32), POOL, SUMS],
        input_output_aliases={11: 1, 12: 2},
        scratch_shapes=[
            pltpu.VMEM((16, 256, 256), jnp.bfloat16),
            pltpu.VMEM((256, 256), jnp.float32),
            pltpu.SMEM((72,), jnp.int32),
            pltpu.SemaphoreType.DMA((4,)),
            pltpu.SemaphoreType.DMA((4,)),
        ],
        compiler_params=pltpu.CompilerParams(vmem_limit_bytes=8 * MIB),
        cost_estimate=pl.CostEstimate(
            flops=80 * 2 * 256 * 256 * 1024, bytes_accessed=8 * MIB, transcendentals=0
        ),
    )(idx, wts, when, dsum, vrow, vcol, slot, *pieces, pool, sums)[0]


def lookup(table, rows, cols):
    ids = jnp.arange(32, dtype=jnp.int32)
    pick = (rows[:, None, None] == ids[None, :, None]) & (
        cols[:, None, None] == ids[None, None, :]
    )
    return jnp.sum(jnp.where(pick, table[None], 0.0), axis=(1, 2))


def coupling(table, orb, cpl):
    i, j = orb[:, 0, None], orb[:, 1, None]
    k, l = cpl[:, :, 0], cpl[:, :, 1]
    first = (l == j) & (k != i)
    second = (k == i) & (l != j)
    rows = jnp.where(first, i, j) + jnp.zeros_like(k)
    cols = jnp.where(first, k, l)
    value = lookup(table, rows.reshape(-1), cols.reshape(-1)).reshape(k.shape)
    return jnp.where(first | second, value, 0.0).reshape(-1)


def arrival(masks):
    order = [0]
    for mask in masks:
        order = order + [o ^ mask for o in order]
    return order


def found_in(values, order):
    ids = jnp.arange(16, dtype=jnp.int32)
    hit = values[..., None] == jnp.array(order, jnp.int32)
    return jnp.sum(jnp.where(hit, ids, 0), axis=-1)


def tables(metas, fock, orb, cpl, cpl_slot):
    col = lax.axis_index("aux")
    grp = lax.axis_index("grp")
    chosen = jnp.sum(
        jnp.where(jnp.arange(16)[None, :] == grp, metas[:, 160:], 0), axis=1
    )
    pick = chosen[:, None, None] == jnp.arange(16, dtype=jnp.int32)[None, :, None]
    sent = jnp.sum(jnp.where(pick, metas[:, :160].reshape(16, 16, 10), 0), axis=1)
    orb_q, cpl_q = sent[:, :2], sent[:, 2:].reshape(16, 4, 2)

    local = jnp.arange(32, dtype=jnp.int32)
    whole = local // 2 * 32 + col * 2 + local % 2
    select = (whole[:, None] == jnp.arange(512)[None, :]).astype(jnp.bfloat16)
    fock_rows = jnp.dot(select, fock, preferred_element_type=jnp.float32)
    fock_col = lax.dot_general(
        fock_rows.astype(jnp.bfloat16), select, NT, preferred_element_type=jnp.float32
    )
    diag = jnp.sum(jnp.where(local[:, None] == local[None, :], fock_col, 0.0), axis=1)

    orbs = jnp.concatenate([orb, orb_q, cpl_q.reshape(64, 2)], axis=0)
    at = orbs[:, :, None] == local[None, None, :]
    dsum = jnp.sum(jnp.where(at, diag[None, None, :], 0.0), axis=2)
    dsum = dsum[:, 0] + dsum[:, 1]
    wts = jnp.concatenate([coupling(fock_col, orb, cpl), coupling(fock_col, orb_q, cpl_q)])

    flat = orbs.T.reshape(192)
    offset = (flat // 2) ^ grp
    spot = jnp.stack([found_in(offset, arrival(masks)) for masks in MASKS])
    slot = found_in(cpl_slot.reshape(64) ^ grp, arrival(MASKS[0]))
    last = jnp.max(spot, axis=0)
    ready = jnp.maximum(last[32:96], last[128:192]) < 12
    when = jnp.where(wts[64:] != 0.0, jnp.where(ready, 1, 2), 0).astype(jnp.int32)
    return spot * 2 + flat % 2, wts, when, slot, dsum


def swap(block, mask):
    return lax.ppermute(block, "grp", [(g, g ^ mask) for g in range(16)])


def join_kernel(*refs):
    held, got, joined = refs[:4], refs[4:8], refs[8:12]
    whole, in_sems, out_sems = refs[12:16], refs[16], refs[17]
    count = held[0].shape[0]

    def in_copies(q):
        return [
            pltpu.make_async_copy(
                source[q], whole[q].at[pl.ds(part * count, count)], in_sems.at[2 * q + part]
            )
            for part, source in enumerate((held, got))
        ]

    copies = [in_copies(q) for q in range(4)]
    outs = [pltpu.make_async_copy(whole[q], joined[q], out_sems.at[q]) for q in range(4)]
    for pair in copies:
        for copy in pair:
            copy.start()
    for pair, out in zip(copies, outs):
        for copy in pair:
            copy.wait()
        out.start()
    for out in outs:
        out.wait()


def join(held, got, grant):
    count, rows, columns = held[0].shape
    shape = (2 * count, rows, columns)
    return pl.pallas_call(
        join_kernel,
        in_specs=[HBM] * 8,
        out_specs=[HBM] * 4,
        out_shape=[jax.ShapeDtypeStruct(shape, jnp.bfloat16)] * 4,
        scratch_shapes=[pltpu.VMEM(shape, jnp.bfloat16)] * 4
        + [pltpu.SemaphoreType.DMA((8,)), pltpu.SemaphoreType.DMA((4,))],
        compiler_params=pltpu.CompilerParams(vmem_limit_bytes=grant * MIB),
        cost_estimate=pl.CostEstimate(
            flops=0, bytes_accessed=16 * count * rows * columns * 2, transcendentals=0
        ),
    )(*held, *got)


def stage_kernel(*refs):
    held, staged = refs[:4], refs[4:8]
    part, in_sems, out_sems = refs[8:12], refs[12], refs[13]
    ins = [pltpu.make_async_copy(held[q], part[q], in_sems.at[q]) for q in range(4)]
    outs = [
        pltpu.make_async_copy(part[q], staged[q].at[pl.ds(0, 2)], out_sems.at[q]) for q in range(4)
    ]
    for copy in ins:
        copy.start()
    for copy, out in zip(ins, outs):
        copy.wait()
        out.start()
    for out in outs:
        out.wait()


def fill_kernel(*refs):
    got, whole = refs[:4], refs[8:12]
    part, in_sems, out_sems = refs[12:16], refs[16], refs[17]
    ins = [pltpu.make_async_copy(got[q], part[q], in_sems.at[q]) for q in range(4)]
    outs = [
        pltpu.make_async_copy(part[q], whole[q].at[pl.ds(2, 2)], out_sems.at[q]) for q in range(4)
    ]
    for copy in ins:
        copy.start()
    for copy, out in zip(ins, outs):
        copy.wait()
        out.start()
    for out in outs:
        out.wait()


def half_call(kernel, blocks, staged):
    shape = (4, *blocks[0].shape[1:])
    return pl.pallas_call(
        kernel,
        in_specs=[HBM] * (4 + len(staged)),
        out_specs=[HBM] * 4,
        out_shape=[jax.ShapeDtypeStruct(shape, jnp.bfloat16)] * 4,
        input_output_aliases={4 + q: q for q in range(len(staged))},
        scratch_shapes=[pltpu.VMEM(blocks[0].shape, jnp.bfloat16)] * 4
        + [pltpu.SemaphoreType.DMA((4,)), pltpu.SemaphoreType.DMA((4,))],
        compiler_params=pltpu.CompilerParams(vmem_limit_bytes=58 * MIB),
        cost_estimate=pl.CostEstimate(flops=0, bytes_accessed=4 * MIB, transcendentals=0),
    )(*blocks, *staged)


def on_device(
    integrals, metric, fock, virt_energy, send_orb, pair_orb, send_pair, cpl_slot, cpl_orb
):
    rows = integrals.reshape(64, 16, 512).transpose(1, 0, 2)
    rows, pair_orb, cpl_orb, send_pair = lax.optimization_barrier(
        (rows, pair_orb, cpl_orb, send_pair)
    )
    orb = pair_orb // 32 * 2 + pair_orb % 2
    cpl = cpl_orb // 32 * 2 + cpl_orb % 2
    metas = jnp.concatenate([orb, cpl.reshape(16, 8)], axis=1).reshape(1, 160)
    metas = jnp.concatenate([metas, send_pair], axis=1)
    for mask in MASKS[0]:
        metas = jnp.concatenate([metas, swap(metas, mask)], axis=0)

    block = lax.all_to_all(rows, "aux", split_axis=0, concat_axis=0, tiled=True)
    given = (*tables(metas, fock, orb, cpl, cpl_slot), virt_energy[None, :], virt_energy[:, None])
    block, (idx, wts, when, slot, dsum, vrow, vcol) = lax.optimization_barrier((block, given))
    fitted = lax.dot_general(
        block.reshape(1024, 512),
        metric,
        (((0,), (1,)), ((), ())),
        preferred_element_type=jnp.float32,
    ).astype(jnp.bfloat16)
    held = [fitted[None, :, 256 * q : 256 * q + 256] for q in range(4)]
    got = [swap(held[q], MASKS[q][0]) for q in range(4)]
    held = join(held, got, 16)
    got = [swap(held[q], MASKS[q][1]) for q in range(4)]
    held = half_call(fill_kernel, got, half_call(stage_kernel, held, []))
    third = [swap(held[q], MASKS[q][2]) for q in range(4)]
    early = [swap(held[q], MASKS[q][3]) for q in range(4)]
    late = [swap(third[q], MASKS[q][3]) for q in range(4)]
    soon = [x.reshape(8, 256, 256) for three in zip(held, third, early) for x in three]
    pool, sums = early_sums(idx, wts, when, dsum, vrow, vcol, soon)
    late = [x.reshape(8, 256, 256) for x in late]
    return amplitudes(idx, wts, when, dsum, vrow, vcol, slot, late, pool, sums)


def solution(mesh):
    in_specs = (
        P("aux", "grp", None),
        P(),
        P(),
        P(),
        P(("aux", "grp"), None),
        P(("aux", "grp"), None),
        P(("aux", "grp"), None),
        P(("aux", "grp"), None),
        P(("aux", "grp"), None, None),
    )
    out_specs = P(("aux", "grp"), None, None)
    return jax.shard_map(
        on_device, mesh=mesh, in_specs=in_specs, out_specs=out_specs, check_vma=False
    )
```

```python
import jax
import jax.numpy as jnp
from jax import lax
from jax.experimental import pallas as pl
from jax.experimental.pallas import tpu as pltpu
from jax.sharding import PartitionSpec as P

NT = (((1,), (1,)), ((), ()))
MIB = 2**20
UNROLL = 8
MASKS = ((4, 12, 1, 3), (1, 3, 4, 12), (12, 4, 3, 1), (3, 1, 12, 4))


def recip(x):
    r = pl.reciprocal(x, approx=True)
    return r * (2.0 - x * r)


def listed(when, kernel, order):
    def entry(n, count):
        hit = when[n] == kernel

        @pl.when(hit)
        def _():
            order[count] = n

        return count + hit.astype(jnp.int32)

    count = lax.fori_loop(0, 64, entry, 0)
    for k in range(UNROLL):
        order[count + k] = -1
    return (count + UNROLL - 1) // UNROLL


def product(idx, pool, n):
    left = jnp.concatenate([pool[q, idx[q, n]] for q in range(4)], axis=1)
    right = jnp.concatenate([pool[q, idx[q, 96 + n]] for q in range(4)], axis=1)
    return lax.dot_general(left, right, NT, preferred_element_type=jnp.float32)


def add_coupled(idx, wts, dsum, pool, mixed, vsum, order, trips):
    def coupled(g, carry):
        for u in range(UNROLL):
            entry = order[UNROLL * g + u]
            n = jnp.maximum(entry, 0)
            weight = jnp.where(entry >= 0, wts[64 + n], 0.0)
            at = jnp.where(entry >= 0, n, order[0])
            start = -(product(idx, pool, 32 + at) * recip(vsum[...] - dsum[32 + at]))
            rounded = start.astype(jnp.bfloat16).astype(jnp.float32)
            mixed[n // 4] += weight * rounded
        return carry

    lax.fori_loop(0, trips, coupled, 0)


def early_kernel(idx, wts, when, dsum, vrow, vcol, *refs):
    pieces, pool, mixed, vsum, order, sems = refs[:12], *refs[12:]
    copies = [
        pltpu.make_async_copy(
            pieces[3 * q + part], pool.at[q, pl.ds(8 * part, 8)], sems.at[3 * q + part]
        )
        for q in range(4)
        for part in range(3)
    ]
    for copy in copies:
        copy.start()
    trips = listed(when, 1, order)
    vsum[...] = vrow[...] + vcol[...]

    def clear(s, carry):
        mixed[s] = jnp.zeros((256, 256), jnp.float32)
        return carry

    lax.fori_loop(0, 16, clear, 0)
    for copy in copies:
        copy.wait()
    add_coupled(idx, wts, dsum, pool, mixed, vsum, order, trips)


def last_kernel(idx, wts, when, dsum, vrow, vcol, slot, *refs):
    pieces, _, _, out, pool, mixed, amp, vsum, order, sems, out_sems = refs[:4], *refs[4:]
    copies = [
        pltpu.make_async_copy(pieces[q], pool.at[q, pl.ds(24, 8)], sems.at[q]) for q in range(4)
    ]
    for copy in copies:
        copy.start()
    trips = listed(when, 2, order)
    vsum[...] = vrow[...] + vcol[...]
    for copy in copies:
        copy.wait()
    add_coupled(idx, wts, dsum, pool, mixed, vsum, order, trips)

    def out_copy(g):
        rows = pl.ds(UNROLL * g, UNROLL)
        return pltpu.make_async_copy(mixed.at[rows], out.at[rows], out_sems.at[g])

    def own(g, carry):
        for u in range(UNROLL):
            p = UNROLL * g + u
            total = -product(idx, pool, p)
            for e in range(4):
                total += wts[4 * p + e] * amp[slot[4 * p + e]].astype(jnp.float32)
            mixed[p] = total * recip(vsum[...] - dsum[p])
        out_copy(g).start()
        return carry

    def finish(g, carry):
        out_copy(g).wait()
        return carry

    for s in range(16):
        value = (mixed[s] - product(idx, pool, 16 + s)) * recip(vsum[...] - dsum[16 + s])
        amp[s] = value.astype(jnp.bfloat16)
    lax.fori_loop(0, 16 // UNROLL, own, 0)
    lax.fori_loop(0, 16 // UNROLL, finish, 0)


SMEM = pl.BlockSpec(memory_space=pltpu.SMEM)
VMEM = pl.BlockSpec(memory_space=pltpu.VMEM)
HBM = pl.BlockSpec(memory_space=pl.ANY)


POOL = pltpu.VMEM((4, 32, 256, 256), jnp.bfloat16)
SUMS = pltpu.VMEM((16, 256, 256), jnp.float32)


def early_sums(idx, wts, when, dsum, vrow, vcol, pieces):
    return pl.pallas_call(
        early_kernel,
        in_specs=[SMEM] * 4 + [VMEM] * 2 + [HBM] * 12,
        out_specs=[VMEM] * 2,
        out_shape=[POOL, SUMS],
        scratch_shapes=[
            pltpu.VMEM((256, 256), jnp.float32),
            pltpu.SMEM((72,), jnp.int32),
            pltpu.SemaphoreType.DMA((12,)),
        ],
        compiler_params=pltpu.CompilerParams(vmem_limit_bytes=36 * MIB),
        cost_estimate=pl.CostEstimate(
            flops=20 * 2 * 256 * 256 * 1024, bytes_accessed=12 * MIB, transcendentals=0
        ),
    )(idx, wts, when, dsum, vrow, vcol, *pieces)


def amplitudes(idx, wts, when, dsum, vrow, vcol, slot, pieces, pool, sums):
    return pl.pallas_call(
        last_kernel,
        in_specs=[SMEM] * 4 + [VMEM] * 2 + [SMEM] + [HBM] * 4 + [VMEM] * 2,
        out_specs=[HBM] + [VMEM] * 2,
        out_shape=[jax.ShapeDtypeStruct((16, 256, 256), jnp.float32), POOL, SUMS],
        input_output_aliases={11: 1, 12: 2},
        scratch_shapes=[
            pltpu.VMEM((16, 256, 256), jnp.bfloat16),
            pltpu.VMEM((256, 256), jnp.float32),
            pltpu.SMEM((72,), jnp.int32),
            pltpu.SemaphoreType.DMA((4,)),
            pltpu.SemaphoreType.DMA((4,)),
        ],
        compiler_params=pltpu.CompilerParams(vmem_limit_bytes=8 * MIB),
        cost_estimate=pl.CostEstimate(
            flops=80 * 2 * 256 * 256 * 1024, bytes_accessed=8 * MIB, transcendentals=0
        ),
    )(idx, wts, when, dsum, vrow, vcol, slot, *pieces, pool, sums)[0]


def lookup(table, rows, cols):
    ids = jnp.arange(32, dtype=jnp.int32)
    pick = (rows[:, None, None] == ids[None, :, None]) & (
        cols[:, None, None] == ids[None, None, :]
    )
    return jnp.sum(jnp.where(pick, table[None], 0.0), axis=(1, 2))


def coupling(table, orb, cpl):
    i, j = orb[:, 0, None], orb[:, 1, None]
    k, l = cpl[:, :, 0], cpl[:, :, 1]
    first = (l == j) & (k != i)
    second = (k == i) & (l != j)
    rows = jnp.where(first, i, j) + jnp.zeros_like(k)
    cols = jnp.where(first, k, l)
    value = lookup(table, rows.reshape(-1), cols.reshape(-1)).reshape(k.shape)
    return jnp.where(first | second, value, 0.0).reshape(-1)


def arrival(masks):
    order = [0]
    for mask in masks:
        order = order + [o ^ mask for o in order]
    return order


def found_in(values, order):
    ids = jnp.arange(16, dtype=jnp.int32)
    hit = values[..., None] == jnp.array(order, jnp.int32)
    return jnp.sum(jnp.where(hit, ids, 0), axis=-1)


def tables(metas, fock, orb, cpl, cpl_slot):
    col = lax.axis_index("aux")
    grp = lax.axis_index("grp")
    chosen = jnp.sum(
        jnp.where(jnp.arange(16)[None, :] == grp, metas[:, 160:], 0), axis=1
    )
    pick = chosen[:, None, None] == jnp.arange(16, dtype=jnp.int32)[None, :, None]
    sent = jnp.sum(jnp.where(pick, metas[:, :160].reshape(16, 16, 10), 0), axis=1)
    orb_q, cpl_q = sent[:, :2], sent[:, 2:].reshape(16, 4, 2)

    local = jnp.arange(32, dtype=jnp.int32)
    whole = local // 2 * 32 + col * 2 + local % 2
    select = (whole[:, None] == jnp.arange(512)[None, :]).astype(jnp.bfloat16)
    fock_rows = jnp.dot(select, fock, preferred_element_type=jnp.float32)
    fock_col = lax.dot_general(
        fock_rows.astype(jnp.bfloat16), select, NT, preferred_element_type=jnp.float32
    )
    diag = jnp.sum(jnp.where(local[:, None] == local[None, :], fock_col, 0.0), axis=1)

    orbs = jnp.concatenate([orb, orb_q, cpl_q.reshape(64, 2)], axis=0)
    at = orbs[:, :, None] == local[None, None, :]
    dsum = jnp.sum(jnp.where(at, diag[None, None, :], 0.0), axis=2)
    dsum = dsum[:, 0] + dsum[:, 1]
    wts = jnp.concatenate([coupling(fock_col, orb, cpl), coupling(fock_col, orb_q, cpl_q)])

    flat = orbs.T.reshape(192)
    offset = (flat // 2) ^ grp
    spot = jnp.stack([found_in(offset, arrival(masks)) for masks in MASKS])
    slot = found_in(cpl_slot.reshape(64) ^ grp, arrival(MASKS[0]))
    last = jnp.max(spot, axis=0)
    ready = jnp.maximum(last[32:96], last[128:192]) < 12
    when = jnp.where(wts[64:] != 0.0, jnp.where(ready, 1, 2), 0).astype(jnp.int32)
    return spot * 2 + flat % 2, wts, when, slot, dsum


def swap(block, mask):
    return lax.ppermute(block, "grp", [(g, g ^ mask) for g in range(16)])


def join_kernel(*refs):
    held, got, joined = refs[:4], refs[4:8], refs[8:12]
    whole, in_sems, out_sems = refs[12:16], refs[16], refs[17]
    count = held[0].shape[0]

    def in_copies(q):
        return [
            pltpu.make_async_copy(
                source[q], whole[q].at[pl.ds(part * count, count)], in_sems.at[2 * q + part]
            )
            for part, source in enumerate((held, got))
        ]

    copies = [in_copies(q) for q in range(4)]
    outs = [pltpu.make_async_copy(whole[q], joined[q], out_sems.at[q]) for q in range(4)]
    for pair in copies:
        for copy in pair:
            copy.start()
    for pair, out in zip(copies, outs):
        for copy in pair:
            copy.wait()
        out.start()
    for out in outs:
        out.wait()


def join(held, got, grant):
    count, rows, columns = held[0].shape
    shape = (2 * count, rows, columns)
    return pl.pallas_call(
        join_kernel,
        in_specs=[HBM] * 8,
        out_specs=[HBM] * 4,
        out_shape=[jax.ShapeDtypeStruct(shape, jnp.bfloat16)] * 4,
        scratch_shapes=[pltpu.VMEM(shape, jnp.bfloat16)] * 4
        + [pltpu.SemaphoreType.DMA((8,)), pltpu.SemaphoreType.DMA((4,))],
        compiler_params=pltpu.CompilerParams(vmem_limit_bytes=grant * MIB),
        cost_estimate=pl.CostEstimate(
            flops=0, bytes_accessed=16 * count * rows * columns * 2, transcendentals=0
        ),
    )(*held, *got)


def stage_kernel(*refs):
    held, staged = refs[:4], refs[4:8]
    part, in_sems, out_sems = refs[8:12], refs[12], refs[13]
    ins = [pltpu.make_async_copy(held[q], part[q], in_sems.at[q]) for q in range(4)]
    outs = [
        pltpu.make_async_copy(part[q], staged[q].at[pl.ds(0, 2)], out_sems.at[q]) for q in range(4)
    ]
    for copy in ins:
        copy.start()
    for copy, out in zip(ins, outs):
        copy.wait()
        out.start()
    for out in outs:
        out.wait()


def fill_kernel(*refs):
    got, whole = refs[:4], refs[8:12]
    part, in_sems, out_sems = refs[12:16], refs[16], refs[17]
    ins = [pltpu.make_async_copy(got[q], part[q], in_sems.at[q]) for q in range(4)]
    outs = [
        pltpu.make_async_copy(part[q], whole[q].at[pl.ds(2, 2)], out_sems.at[q]) for q in range(4)
    ]
    for copy in ins:
        copy.start()
    for copy, out in zip(ins, outs):
        copy.wait()
        out.start()
    for out in outs:
        out.wait()


def half_call(kernel, blocks, staged):
    shape = (4, *blocks[0].shape[1:])
    return pl.pallas_call(
        kernel,
        in_specs=[HBM] * (4 + len(staged)),
        out_specs=[HBM] * 4,
        out_shape=[jax.ShapeDtypeStruct(shape, jnp.bfloat16)] * 4,
        input_output_aliases={4 + q: q for q in range(len(staged))},
        scratch_shapes=[pltpu.VMEM(blocks[0].shape, jnp.bfloat16)] * 4
        + [pltpu.SemaphoreType.DMA((4,)), pltpu.SemaphoreType.DMA((4,))],
        compiler_params=pltpu.CompilerParams(vmem_limit_bytes=58 * MIB),
        cost_estimate=pl.CostEstimate(flops=0, bytes_accessed=4 * MIB, transcendentals=0),
    )(*blocks, *staged)


def on_device(
    integrals, metric, fock, virt_energy, send_orb, pair_orb, send_pair, cpl_slot, cpl_orb
):
    rows = integrals.reshape(64, 16, 512).transpose(1, 0, 2)
    rows, pair_orb, cpl_orb, send_pair = lax.optimization_barrier(
        (rows, pair_orb, cpl_orb, send_pair)
    )
    orb = pair_orb // 32 * 2 + pair_orb % 2
    cpl = cpl_orb // 32 * 2 + cpl_orb % 2
    metas = jnp.concatenate([orb, cpl.reshape(16, 8)], axis=1).reshape(1, 160)
    metas = jnp.concatenate([metas, send_pair], axis=1)
    for mask in MASKS[0]:
        metas = jnp.concatenate([metas, swap(metas, mask)], axis=0)

    block = lax.all_to_all(rows, "aux", split_axis=0, concat_axis=0, tiled=True)
    given = (*tables(metas, fock, orb, cpl, cpl_slot), virt_energy[None, :], virt_energy[:, None])
    block, (idx, wts, when, slot, dsum, vrow, vcol) = lax.optimization_barrier((block, given))
    fitted = lax.dot_general(
        block.reshape(1024, 512),
        metric,
        (((0,), (1,)), ((), ())),
        preferred_element_type=jnp.float32,
    ).astype(jnp.bfloat16)
    held = [fitted[None, :, 256 * q : 256 * q + 256] for q in range(4)]
    got = [swap(held[q], MASKS[q][0]) for q in range(4)]
    held = join(held, got, 16)
    got = [swap(held[q], MASKS[q][1]) for q in range(4)]
    held = half_call(fill_kernel, got, half_call(stage_kernel, held, []))
    third = [swap(held[q], MASKS[q][2]) for q in range(4)]
    early = [swap(held[q], MASKS[q][3]) for q in range(4)]
    late = [swap(third[q], MASKS[q][3]) for q in range(4)]
    soon = [x.reshape(8, 256, 256) for three in zip(held, third, early) for x in three]
    pool, sums = early_sums(idx, wts, when, dsum, vrow, vcol, soon)
    late = [x.reshape(8, 256, 256) for x in late]
    return amplitudes(idx, wts, when, dsum, vrow, vcol, slot, late, pool, sums)


def solution(mesh):
    in_specs = (
        P("aux", "grp", None),
        P(),
        P(),
        P(),
        P(("aux", "grp"), None),
        P(("aux", "grp"), None),
        P(("aux", "grp"), None),
        P(("aux", "grp"), None),
        P(("aux", "grp"), None, None),
    )
    out_specs = P(("aux", "grp"), None, None)
    return jax.shard_map(
        on_device, mesh=mesh, in_specs=in_specs, out_specs=out_specs, check_vma=False
    )
```
